32 devices in a mesh: req: 8 (over y, x, core), rep: 4 (over z).
Axes of the slice: x: 2, y: 2, z: 4, core: 2. Of those that a mesh axis runs over, the one named last changes fastest.
Arguments:
- tokens: bfloat16 [32, 2, 2048], P('req'), may hold values from -6 to 6
- norm_gains: float32 [2, 2048], replicated, may hold values from 0.1 to 1.9
- w_kv: bfloat16 [2048, 2, 2048], P(None, None, 'rep'), may hold values from -0.125 to 0.125
- w_query: bfloat16 [8, 2048, 2048], P('req', None, 'rep'), may hold values from -0.125 to 0.125
- w_out: bfloat16 [8, 2048, 2048], P('req', 'rep'), may hold values from -0.5 to 0.5
- w_gate: bfloat16 [8, 2048, 5632], P('req', None, 'rep'), may hold values from -0.125 to 0.125
- w_up: bfloat16 [8, 2048, 5632], P('req', None, 'rep'), may hold values from -0.125 to 0.125
- w_down: bfloat16 [8, 5632, 2048], P('req', 'rep'), may hold values from -0.078125 to 0.078125
- kv_pages: bfloat16 [2048, 16, 2, 2048], P('req', None, None, 'rep'), may hold values from -80 to 80
- page_table: int32 [32, 64], P('req'), may hold values from 0 to 255, as said below
- cache_len: int32 [32], P('req'), may hold values from 1 to 1024
- route_ids: int32 [32, 2, 2, 2], P('req'), may hold values from 0 to 7, all different within a row
- route_gates: bfloat16 [32, 2, 2, 2], P('req'), may hold values from 0.19921875 to 1
- new_slot: int32 [32], P('req'), may hold values from 0 to 31, each once
Outputs:
- layer_out: bfloat16 [32, 2, 2048], P('req')
The draws below stay inside these ranges and needn't reach their ends.
Inputs may be any that keep to these rules, and one draw needn't show every extreme that they name: `page_table`: row i lists 64 distinct pages of the pool of the device that holds request i; two requests of one device share no page.
All inputs are finite; a program needn't handle non-finite values.
Results may differ from the reference program's by a relative error of at most 0.022.
Values may be sent and summed in bfloat16 or wider, within the bound.
A program may use at most 128 MiB of HBM per device.

```python
import math
import jax
import jax.numpy as jnp
from jax import lax

D = 2048
H = 16
HD = 128
EXPERTS = 8
FFW = 5632
REQ_DEV = 4
PAGE = 16
MAXP = 64
PAGES_DEV = 256
HOLDERS = 1
REQUESTS = 32
POOL = 2048
N_REQ = 8
N_REP = 4


def draw_kv_pages(key, part):
    normal_key = jax.random.fold_in(key, 0)
    values = jnp.clip(jax.random.normal(normal_key, (POOL, PAGE, 2, H * HD), jnp.float32), -4.0, 4.0)
    return values.astype(jnp.bfloat16)


def draw_page_table(key, part):
    owners = REQUESTS // REQ_DEV
    orders = jax.vmap(lambda owner_key: jax.random.permutation(owner_key, PAGES_DEV))(jax.random.split(key, owners))
    return orders.reshape(REQUESTS, MAXP).astype(jnp.int32)


def draw_cache_len(key, part):
    subkeys = jax.random.split(key, 4)
    exponent = jax.random.randint(subkeys[0], (REQUESTS,), 4, 11)
    ceiling = jnp.left_shift(jnp.ones((REQUESTS,), jnp.int32), exponent)
    lengths = 1 + jax.random.randint(subkeys[1], (REQUESTS,), 0, ceiling)
    longest = jax.random.randint(subkeys[2], (), 0, REQUESTS)
    shortest = (longest + 1 + jax.random.randint(subkeys[3], (), 0, REQUESTS - 1)) % REQUESTS
    position = jnp.arange(REQUESTS, dtype=jnp.int32)
    lengths = jnp.minimum(lengths, MAXP * PAGE)
    lengths = jnp.where(position == longest, MAXP * PAGE, lengths)
    lengths = jnp.where(position == shortest, 1, lengths)
    return lengths.astype(jnp.int32)


def levels(rng, dims, shards, least, top_value):
    def one(dim, parts):
        draws = jax.random.uniform(jax.random.fold_in(jax.random.fold_in(rng, 6), dim), (parts,), jnp.float32, least / len(shards), top_value / len(shards))
        return jnp.repeat(jnp.exp(draws), dims[dim] // parts).reshape((-1,) + (1,) * (len(dims) - dim - 1))

    level = one(*shards[0])
    for cut in shards[1:]:
        level = level * one(*cut)
    return level


def different_ones(rng, rows, count, top, lift):
    ranking = jax.random.permutation(jax.random.fold_in(rng, 1), count)
    pull = ranking
    for power in range(3):
        pull = pull * pull // count
    pull = pull * lift // count
    lots = jax.random.randint(jax.random.fold_in(rng, 2), (rows, count), 0, 4096) + pull
    sure = jax.random.permutation(jax.random.fold_in(rng, 3), rows)[jnp.arange(count) % rows]
    lots = jnp.where(jnp.arange(rows)[:, None] == sure[None, :], 1 << 14, lots)
    score = lots * count + jnp.arange(count)
    return lax.top_k(score.astype(jnp.int32), top)[1].astype(jnp.int32)


def normal_values(own_key, extent, scale, bound, shards=(), kind=jnp.bfloat16):
    values = scale * jax.random.normal(own_key, extent, jnp.float32)
    if shards:
        values = values * levels(own_key, extent, shards, -0.22, 0.18)
    return jnp.clip(values, -bound, bound).astype(kind)


def setup_inputs(seed: int = 0) -> dict:
    key_of = jax.random.split(jax.random.key(seed), 15)
    tokens = normal_values(key_of[0], (REQUESTS, 2, D), 1.0, 6.0, ((0, 8),))
    norm_gains = jnp.clip(1.0 + 0.18 * jax.random.normal(key_of[1], (2, D), jnp.float32), 0.1, 1.9)
    w_kv = normal_values(key_of[2], (D, 2, H * HD), D ** -0.5, 0.125, ((2, 4),))
    w_query = normal_values(key_of[3], (EXPERTS * HOLDERS, D, H * HD // HOLDERS), D ** -0.5, 0.125, ((0, 8), (2, 4)))
    w_out = normal_values(key_of[4], (EXPERTS * HOLDERS, H * HD // HOLDERS, D), HD ** -0.5, 0.5, ((0, 8), (1, 4)))
    w_gate = normal_values(key_of[5], (EXPERTS * HOLDERS, D, FFW // HOLDERS), D ** -0.5, 0.125, ((0, 8), (2, 4)))
    w_up = normal_values(key_of[6], (EXPERTS * HOLDERS, D, FFW // HOLDERS), D ** -0.5, 0.125, ((0, 8), (2, 4)))
    w_down = normal_values(key_of[7], (EXPERTS * HOLDERS, FFW // HOLDERS, D), FFW ** -0.5, 0.078125, ((0, 8), (1, 4)))
    kv_pages = draw_kv_pages(jax.random.fold_in(key_of[14], 71), 0)
    page_table = draw_page_table(jax.random.fold_in(key_of[14], 71), 0)
    cache_len = draw_cache_len(jax.random.fold_in(key_of[14], 71), 0)
    route_ids = different_ones(key_of[11], REQUESTS * 2 * 2, EXPERTS, 2, 4096).reshape((REQUESTS, 2, 2, 2))
    route_gates = jnp.clip(0.19921875 + 0.80078125 * jax.random.uniform(key_of[12], (REQUESTS, 2, 2, 2), jnp.float32) ** levels(key_of[12], (REQUESTS, 2, 2, 2), ((0, 8),), -0.2, 0.2), 0.19921875, 1.0).astype(jnp.bfloat16)
    new_slot = jax.random.permutation(key_of[13], REQUESTS).astype(jnp.int32)
    return dict(tokens=tokens, norm_gains=norm_gains, w_kv=w_kv, w_query=w_query, w_out=w_out, w_gate=w_gate, w_up=w_up, w_down=w_down, kv_pages=kv_pages, page_table=page_table, cache_len=cache_len, route_ids=route_ids, route_gates=route_gates, new_slot=new_slot)


EPSILON = 1e-06
MASKED = -1e+30

def normalize(values, gain_row):
    scaling = lax.rsqrt(lax.optimization_barrier(jnp.mean(values * values, axis=-1, keepdims=True)) + EPSILON)
    return (values * scaling * gain_row).astype(jnp.bfloat16)

def attend(queries, cache_keys, cache_values, lengths, extra_keys, extra_values, extra_live):
    inv_scale = 1.0 / math.sqrt(queries.shape[-1])
    query_wide = queries.astype(jnp.float32)
    cache_scores = jnp.einsum('jskhc,jlhc->jskhl', query_wide, cache_keys.astype(jnp.float32)) * inv_scale
    alive_mask = jnp.arange(cache_keys.shape[1], dtype=jnp.int32)[None, :] < lengths[:, None]
    cache_scores = jnp.where(alive_mask[:, None, None, None, :], cache_scores, MASKED)
    extra_scores = jnp.einsum('jskhc,jxhc->jskhx', query_wide, extra_keys.astype(jnp.float32)) * inv_scale
    extra_scores = jnp.where(extra_live[None, :, None, None, :], extra_scores, MASKED)
    highest = jnp.maximum(lax.optimization_barrier(jnp.max(cache_scores, axis=-1)), lax.optimization_barrier(jnp.max(extra_scores, axis=-1)))[..., None]
    cache_exp = jnp.exp(cache_scores - highest)
    extra_exp = jnp.exp(extra_scores - highest)
    denominator = (lax.optimization_barrier(jnp.sum(cache_exp, axis=-1)) + lax.optimization_barrier(jnp.sum(extra_exp, axis=-1)))[..., None]
    cache_weight = (cache_exp / denominator).astype(jnp.bfloat16)
    extra_weight = (extra_exp / denominator).astype(jnp.bfloat16)
    mixture = jnp.einsum('jskhl,jlhc->jskhc', cache_weight.astype(jnp.float32), cache_values.astype(jnp.float32))
    mixture = mixture + jnp.einsum('jskhx,jxhc->jskhc', extra_weight.astype(jnp.float32), extra_values.astype(jnp.float32))
    return mixture.astype(jnp.bfloat16)

def reference(tokens, norm_gains, w_kv, w_query, w_out, w_gate, w_up, w_down, kv_pages, page_table, cache_len, route_ids, route_gates, new_slot):
    all_rows = tokens.shape[0]
    holders = N_REQ // EXPERTS
    heads_dev = H // (holders * N_REP)
    units_dev = FFW // (holders * N_REP)
    inner = H * HD
    query_full = w_query.reshape(EXPERTS, holders, D, N_REP, heads_dev * HD).transpose(0, 2, 3, 1, 4).reshape(EXPERTS, D, inner)
    out_full = w_out.reshape(EXPERTS, holders, N_REP, heads_dev * HD, D).transpose(0, 2, 1, 3, 4).reshape(EXPERTS, inner, D)
    gate_full = w_gate.reshape(EXPERTS, holders, D, N_REP, units_dev).transpose(0, 2, 1, 3, 4).reshape(EXPERTS, D, FFW)
    up_full = w_up.reshape(EXPERTS, holders, D, N_REP, units_dev).transpose(0, 2, 1, 3, 4).reshape(EXPERTS, D, FFW)
    down_full = w_down.reshape(EXPERTS, FFW, D)
    position = jnp.arange(all_rows, dtype=jnp.int32)
    inverse = jnp.zeros((all_rows,), jnp.int32).at[new_slot].set(position)
    inputs = tokens.astype(jnp.float32)
    normed = normalize(inputs, norm_gains[0])
    fresh = jnp.einsum('bsd,dtc->bstc', normed.astype(jnp.float32), w_kv.astype(jnp.float32)).astype(jnp.bfloat16)
    extra_kv = jnp.stack([fresh[:, 0], fresh[new_slot, 1]], axis=1)
    all_queries = jnp.einsum('bsd,edc->bsec', normed.astype(jnp.float32), query_full.astype(jnp.float32))
    experts_row = jnp.arange(EXPERTS, dtype=jnp.int32)
    attn_ids = route_ids[:, 0]
    chosen = (attn_ids[..., None] == experts_row).astype(jnp.float32)
    picked = jnp.einsum('bske,bsec->bskc', chosen, all_queries).astype(jnp.bfloat16)
    old_queries = jnp.stack([picked[:, 0], picked[new_slot, 1]], axis=1)
    tables = (position // REQ_DEV)[:, None] * PAGES_DEV + page_table
    extra_live = jnp.array([[True, False], [True, True]])

    def one_request(item):
        query_rows, table_row, length, extra_row = item
        block = kv_pages[table_row].reshape(-1, 2, H, HD)
        extra_row = extra_row.reshape(2, 2, H, HD)
        result = attend(query_rows.reshape(1, 2, 2, H, HD), block[None, :, 0], block[None, :, 1], length[None], extra_row[None, :, 0], extra_row[None, :, 1], extra_live)
        return result[0]
    outcome = lax.map(one_request, (old_queries, tables, cache_len, extra_kv))
    outcome = outcome.reshape(all_rows, 2, 2, inner)
    answers = jnp.stack([outcome[:, 0], outcome[inverse, 1]], axis=1)
    flat_answers = answers.reshape(-1, inner)
    attn_gates = route_gates[:, 0].astype(jnp.float32)
    mixture = jnp.zeros((all_rows, 2, D), jnp.float32)
    for expert in range(EXPERTS):
        projected = jnp.dot(flat_answers, out_full[expert], preferred_element_type=jnp.float32).reshape(all_rows, 2, 2, D)
        weight = jnp.where(attn_ids == expert, attn_gates, 0.0)
        mixture = mixture + lax.optimization_barrier(jnp.sum(projected * weight[..., None], axis=2))
    hidden = inputs + mixture
    hidden_normed = normalize(hidden, norm_gains[1]).reshape(-1, D)
    ffn_ids = route_ids[:, 1]
    ffn_gates = route_gates[:, 1].astype(jnp.float32)
    feed = jnp.zeros((all_rows, 2, D), jnp.float32)
    for expert in range(EXPERTS):
        gate_part = jnp.dot(hidden_normed, gate_full[expert], preferred_element_type=jnp.float32)
        up_part = jnp.dot(hidden_normed, up_full[expert], preferred_element_type=jnp.float32)
        active = (jax.nn.silu(gate_part) * up_part).astype(jnp.bfloat16)
        projected = jnp.dot(active, down_full[expert], preferred_element_type=jnp.float32).reshape(all_rows, 2, D)
        weight = lax.optimization_barrier(jnp.sum(jnp.where(ffn_ids == expert, ffn_gates, 0.0), axis=-1))
        feed = feed + projected * weight[..., None]
    return (hidden + feed).astype(jnp.bfloat16)
```

```python
import math

import jax
import jax.numpy as jnp
from jax import lax
from jax.sharding import PartitionSpec as P

HD = 128
EXPERTS = 8
EPSILON = 1e-06
MASKED = -1e30


def normalize(values, gain_row):
    scaling = lax.rsqrt(jnp.mean(values * values, axis=-1, keepdims=True) + EPSILON)
    return (values * scaling * gain_row).astype(jnp.bfloat16)


def swap(blocks, axis):
    return lax.all_to_all(blocks, axis, split_axis=0, concat_axis=0, tiled=True)


def share_all(block, axis):
    return swap(jnp.broadcast_to(block[None], (lax.axis_size(axis),) + block.shape), axis)


def dot32(spec, left, right):
    return jnp.einsum(spec, left, right, preferred_element_type=jnp.float32)


def combine(partial):
    count = lax.axis_size("req")
    blocks = partial.astype(jnp.bfloat16).reshape((count, -1) + partial.shape[1:])
    mine = jnp.sum(swap(blocks, "req").astype(jnp.float32), axis=0).astype(jnp.bfloat16)
    return jnp.sum(share_all(mine, "rep").astype(jnp.float32), axis=0)


def pool_mask(page_table, cache_len, pages, page):
    requests, listed = page_table.shape
    start = jnp.arange(listed, dtype=jnp.int32)[None, :] * page
    count = jnp.clip(cache_len[:, None] - start, 0, page)
    owner = page_table[:, :, None] == jnp.arange(pages, dtype=jnp.int32)
    held = jnp.sum(jnp.where(owner, count[:, :, None], 0), axis=1)
    alive = jnp.arange(page, dtype=jnp.int32)[None, None, :] < held[:, :, None]
    return alive.reshape(requests, pages * page)


def attend(queries, keys, values, alive, extra_keys, extra_values):
    inv_scale = 1.0 / math.sqrt(queries.shape[-1])
    rows, steps, picks, heads, _ = queries.shape
    cache = dot32("jskhc,nhc->hjskn", queries, keys) * inv_scale
    cache = jnp.where(alive[None, :, None, None, :], cache, MASKED)
    extra = dot32("jskhc,jxhc->hjskx", queries, extra_keys) * inv_scale
    seen = jnp.arange(2)[None, :] <= jnp.arange(steps)[:, None]
    extra = jnp.where(seen[None, None, :, None, :], extra, MASKED)
    highest = jnp.maximum(jnp.max(cache, axis=-1), jnp.max(extra, axis=-1))[..., None]
    cache_exp = jnp.exp(cache - highest)
    extra_exp = jnp.exp(extra - highest)
    total = (jnp.sum(cache_exp, axis=-1) + jnp.sum(extra_exp, axis=-1))[..., None]
    cache_weight = (cache_exp / total).astype(jnp.bfloat16)
    extra_weight = (extra_exp / total).astype(jnp.bfloat16)
    mixture = dot32("hjskn,nhc->jskhc", cache_weight, values)
    mixture = mixture + dot32("hjskx,jxhc->jskhc", extra_weight, extra_values)
    return mixture.astype(jnp.bfloat16)


def shards(
    tokens,
    norm_gains,
    w_kv,
    w_query,
    w_out,
    w_gate,
    w_up,
    w_down,
    kv_pages,
    page_table,
    cache_len,
    route_ids,
    route_gates,
    new_slot,
):
    rows_dev, steps, width = tokens.shape
    count = lax.axis_size("req")
    all_rows = rows_dev * count
    holders = count // EXPERTS
    expert = lax.axis_index("req") // holders
    heads_rep = kv_pages.shape[-1] // HD
    heads_dev = w_query.shape[-1] // HD
    pages, page = kv_pages.shape[:2]
    inputs = tokens.astype(jnp.float32)
    normed = normalize(inputs, norm_gains[0])
    payload = jnp.concatenate(
        [
            normed.reshape(rows_dev, steps * width),
            route_ids.reshape(rows_dev, 8).astype(jnp.bfloat16),
            route_gates.reshape(rows_dev, 8),
            new_slot[:, None].astype(jnp.bfloat16),
            jnp.zeros((rows_dev, 111), jnp.bfloat16),
        ],
        axis=1,
    )
    got = share_all(payload, "req").reshape(all_rows, -1)
    base = steps * width
    all_normed = got[:, :base].reshape(all_rows, steps, width)
    ids = got[:, base : base + 8].astype(jnp.int32).reshape(all_rows, 2, 2, 2)
    gates = got[:, base + 8 : base + 16].astype(jnp.float32).reshape(all_rows, 2, 2, 2)
    slot = got[:, base + 16].astype(jnp.int32)
    moved = (slot[:, None] == jnp.arange(all_rows, dtype=jnp.int32)).astype(jnp.bfloat16)
    second = dot32("ib,bd->id", moved, all_normed[:, 1]).astype(jnp.bfloat16)
    rows = jnp.stack([all_normed[:, 0], second], axis=1)
    queries = dot32("bsd,dc->bsc", rows, w_query[0]).astype(jnp.bfloat16)
    arrived = swap(queries.reshape(count, rows_dev, steps, heads_dev * HD), "req")
    arrived = arrived.reshape(EXPERTS, holders, rows_dev, steps, heads_dev, HD)
    own = lax.dynamic_slice_in_dim(rows, lax.axis_index("req") * rows_dev, rows_dev, axis=0)
    fresh = dot32("jsd,dtc->jstc", own, w_kv).astype(jnp.bfloat16)
    fresh = fresh.reshape(rows_dev, 2, 2, heads_rep, HD)
    mine = new_slot[:, None] == jnp.arange(all_rows, dtype=jnp.int32)
    moved_ids = jnp.sum(jnp.where(mine[:, :, None], ids[None, :, 0, 1], 0), axis=1)
    own_ids = jnp.stack([route_ids[:, 0, 0], moved_ids], axis=1)
    chosen = (own_ids[..., None] == jnp.arange(EXPERTS, dtype=jnp.int32)).astype(jnp.bfloat16)
    picked = dot32("jske,egjshc->jskghc", chosen, arrived).astype(jnp.bfloat16)
    picked = picked.reshape(rows_dev, steps, 2, heads_rep, HD)
    keys = kv_pages[:, :, 0].reshape(pages * page, heads_rep, HD)
    values = kv_pages[:, :, 1].reshape(pages * page, heads_rep, HD)
    alive = pool_mask(page_table, cache_len, pages, page)
    result = attend(picked, keys, values, alive, fresh[:, :, 0], fresh[:, :, 1])
    result = result.reshape(rows_dev, steps, 2, holders, heads_dev, HD)
    spread = dot32("jske,jskghc->egjshc", chosen, result).astype(jnp.bfloat16)
    returned = swap(spread.reshape(count, rows_dev, steps, heads_dev * HD), "req")
    returned = returned.reshape(all_rows, steps, heads_dev * HD)
    back = dot32("ib,ic->bc", moved, returned[:, 1]).astype(jnp.bfloat16)
    answers = jnp.stack([returned[:, 0], back], axis=1)
    shares = jnp.sum(jnp.where(ids == expert, gates, 0.0), axis=-1)
    attn = dot32("bsc,cd->bsd", answers, w_out[0]) * shares[:, 0, :, None]
    hidden = inputs + combine(attn)
    hidden_normed = normalize(hidden, norm_gains[1])
    block = share_all(hidden_normed, "req").reshape(all_rows, steps, width)
    gate_part = dot32("bsd,df->bsf", block, w_gate[0])
    up_part = dot32("bsd,df->bsf", block, w_up[0])
    units = (jax.nn.silu(gate_part) * up_part).astype(jnp.bfloat16)
    feed = dot32("bsf,fd->bsd", units, w_down[0]) * shares[:, 1, :, None]
    return (hidden + combine(feed)).astype(jnp.bfloat16)


def solution(mesh):
    in_specs = (
        P("req", None, None),
        P(),
        P(None, None, "rep"),
        P("req", None, "rep"),
        P("req", "rep", None),
        P("req", None, "rep"),
        P("req", None, "rep"),
        P("req", "rep", None),
        P("req", None, None, "rep"),
        P("req", None),
        P("req"),
        P("req", None, None, None),
        P("req", None, None, None),
        P("req"),
    )
    out_specs = P("req", None, None)
    return jax.shard_map(shards, mesh=mesh, in_specs=in_specs, out_specs=out_specs, check_vma=False)
```

```python
import functools
import math

import jax
import jax.numpy as jnp
from jax import lax
from jax.experimental import pallas as pl
from jax.experimental.pallas import tpu as pltpu
from jax.sharding import PartitionSpec as P

HD = 128
EXPERTS = 8
EPSILON = 1e-06
MASKED = -1e30


def pool_mask(page_table, cache_len, pages, page):
    requests, listed = page_table.shape
    start = jnp.arange(listed, dtype=jnp.int32)[None, :] * page
    count = jnp.clip(cache_len[:, None] - start, 0, page)
    owner = page_table[:, :, None] == jnp.arange(pages, dtype=jnp.int32)
    held = jnp.sum(jnp.where(owner, count[:, :, None], 0), axis=1)
    alive = jnp.arange(page, dtype=jnp.int32)[None, None, :] < held[:, :, None]
    return alive.reshape(requests, pages * page)


CHUNK = 4096
MESH = pl.DeviceIdType.MESH


def dot32(left, right):
    return jnp.dot(left, right, preferred_element_type=jnp.float32)


def dot_rows(left, right):
    return lax.dot_general(left, right, (((1,), (1,)), ((), ())), preferred_element_type=jnp.float32)


def iota32(shape, dim):
    return lax.broadcasted_iota(jnp.int32, shape, dim).astype(jnp.float32)


def half_norm(values, gains):
    half = values.shape[0] // 2
    squares = jnp.sum(values * values, axis=-1, keepdims=True)
    mean = (squares[:half] + squares[half:]) / (2.0 * values.shape[1])
    scaling = lax.rsqrt(mean + EPSILON)
    left = jnp.broadcast_to(gains[0:1], (half, values.shape[1]))
    right = jnp.broadcast_to(gains[1:2], (half, values.shape[1]))
    gain = jnp.concatenate([left, right], axis=0)
    return (values * jnp.concatenate([scaling, scaling], axis=0) * gain).astype(jnp.bfloat16)


def whole_rows(buffer):
    count, twice, half_width = buffer.shape
    rows = twice // 2
    wide = buffer[...].astype(jnp.float32)
    left = wide[:, :rows].reshape(count * rows, half_width)
    right = wide[:, rows:].reshape(count * rows, half_width)
    return jnp.concatenate([left, right], axis=1).astype(jnp.bfloat16)


def layer_kernel(
    holders,
    tok_ref,
    gain_ref,
    meta_ref,
    bias_ref,
    kv_ref,
    wkv_ref,
    wq_ref,
    wo_ref,
    wg_ref,
    wu_ref,
    wd_ref,
    out_ref,
    kv_buf,
    wkv_buf,
    chunk_buf,
    stage,
    wq,
    wo,
    wg,
    wu,
    wd,
    act_buf,
    norm1,
    meta,
    q_send,
    q_recv,
    a_send,
    a_recv,
    p_send1,
    p_recv1,
    h_recv1,
    norm2,
    p_send2,
    p_recv2,
    h_recv2,
    weight_sem,
    chunk_sem,
    send_sem,
    recv_sem,
    rep_send_sem,
    rep_recv_sem,
):
    count = norm1.shape[0]
    reps = h_recv1.shape[0]
    rows = meta.shape[1]
    all_rows = count * rows
    half_width = norm1.shape[2]
    head_cols = wq.shape[1]
    heads = kv_buf.shape[0] // 2
    me = lax.axis_index("req")
    rep = lax.axis_index("rep")
    expert = (me // holders).astype(jnp.float32)
    pending = []

    loads = []
    for place, (source, target) in enumerate(
        ((wq_ref, wq), (wo_ref, wo), (wg_ref, wg), (wu_ref, wu), (wd_ref, wd))
    ):
        loads.append(pltpu.make_async_copy(source, target, weight_sem.at[place]))
    loads[0].start()

    barrier = pltpu.get_barrier_semaphore()
    for step in range(1, count):
        peer = lax.rem(me + step, count)
        pl.semaphore_signal(barrier, inc=1, device_id={"req": peer}, device_id_type=MESH)
    for step in range(1, reps):
        peer = lax.rem(rep + step, reps)
        pl.semaphore_signal(barrier, inc=1, device_id={"rep": peer}, device_id_type=MESH)

    def send_req(phase, block_of, target):
        copies = []
        for step in range(1, count):
            peer = lax.rem(me + step, count)
            copy = pltpu.make_async_remote_copy(
                src_ref=block_of(peer),
                dst_ref=target.at[me],
                send_sem=send_sem.at[phase, step],
                recv_sem=recv_sem.at[phase, step],
                device_id={"req": peer},
                device_id_type=MESH,
            )
            copy.start()
            copies.append(copy)
        pending.extend(copies)
        return copies

    def send_rep(phase, target):
        copies = []
        for step in range(1, reps):
            peer = lax.rem(rep + step, reps)
            copy = pltpu.make_async_remote_copy(
                src_ref=target.at[rep],
                dst_ref=target.at[rep],
                send_sem=rep_send_sem.at[phase, step],
                recv_sem=rep_recv_sem.at[phase, step],
                device_id={"rep": peer},
                device_id_type=MESH,
            )
            copy.start()
            copies.append(copy)
        pending.extend(copies)
        return copies

    def arrive(copies):
        for copy in copies:
            copy.wait_recv()

    def split_chunks(source, target, first, last):
        def fetch(index):
            return pltpu.make_async_copy(
                source.at[pl.ds(pl.multiple_of(index * CHUNK, CHUNK), CHUNK)],
                chunk_buf.at[lax.rem(index, 2)],
                chunk_sem.at[lax.rem(index, 2)],
            )

        per_chunk = CHUNK // (2 * heads)
        fetch(jnp.int32(first)).start()

        @pl.loop(first, last)
        def _(index):
            fetch(index).wait()

            @pl.when(index + 1 < last)
            def _():
                fetch(index + 1).start()

            stage[...] = chunk_buf[lax.rem(index, 2)].astype(jnp.float32)
            spot = pl.ds(pl.multiple_of(index * per_chunk, per_chunk), per_chunk)
            for part in range(2 * heads):
                target[part, spot, :] = stage[
                    pl.ds(part, per_chunk, stride=2 * heads), :
                ].astype(jnp.bfloat16)

    inputs = tok_ref[...].astype(jnp.float32)
    norm1[me] = half_norm(inputs, gain_ref[0])
    meta[me] = meta_ref[...]
    pl.semaphore_wait(barrier, count - 1 + reps - 1)
    norm_copies = send_req(0, lambda peer: norm1.at[me], norm1)
    meta_copies = send_req(1, lambda peer: meta.at[me], meta)

    kv_chunks = kv_ref.shape[0] // CHUNK
    wkv_chunks = wkv_ref.shape[0] // CHUNK
    split_chunks(kv_ref, kv_buf, 0, kv_chunks // 2)
    for load in loads[1:]:
        load.start()

    arrive(norm_copies)
    arrive(meta_copies)
    normed = whole_rows(norm1)
    table = meta[...].reshape(all_rows, 128)
    table16 = table.astype(jnp.bfloat16)
    moved = jnp.where(table[:, 0:1] == iota32((all_rows, all_rows), 1), 1.0, 0.0)
    moved = moved.astype(jnp.bfloat16)
    own_moved = jnp.where(meta_ref[:, 0:1] == iota32((rows, all_rows), 1), 1.0, 0.0)
    own_moved = own_moved.astype(jnp.bfloat16)
    pick_lane = jnp.where(iota32((8, 128), 1) == 0.0, 1.0, 0.0).astype(jnp.bfloat16)
    target_row = dot_rows(pick_lane, table16)[0:1]
    moved_back = jnp.where(target_row == iota32((all_rows, all_rows), 0), 1.0, 0.0)
    moved_back = moved_back.astype(jnp.bfloat16)

    loads[0].wait()
    queries = dot32(normed, wq[...]).astype(jnp.bfloat16)
    q_send[...] = dot32(moved, queries).reshape(count, rows, head_cols)
    q_recv[me] = q_send[me]
    q_copies = send_req(2, lambda peer: q_send.at[peer], q_recv)

    split_chunks(wkv_ref, wkv_buf, 0, wkv_chunks)
    own_rows = dot32(own_moved, normed).astype(jnp.bfloat16)
    own_table = dot32(own_moved, table16)
    for part in range(2 * heads):
        fresh = dot32(own_rows, wkv_buf[part])
        padded = jnp.concatenate([fresh, jnp.zeros((128 - rows, HD), jnp.float32)], axis=0)
        kv_buf[part, pl.ds(kv_buf.shape[1] - 128, 128), :] = padded.astype(jnp.bfloat16)
    split_chunks(kv_ref, kv_buf, kv_chunks // 2, kv_chunks)

    arrive(q_copies)
    picked = []
    for k in range(2):
        wanted = own_table[:, 1 + k : 2 + k]
        blocks = []
        for part in range(holders):
            block = jnp.zeros((rows, head_cols), jnp.float32)
            for number in range(EXPERTS):
                arrived = q_recv[number * holders + part]
                block = block + jnp.where(wanted == float(number), arrived, 0.0)
            blocks.append(block)
        picked.append(jnp.concatenate(blocks, axis=1) if holders > 1 else blocks[0])

    bias = bias_ref[...]
    bias = jnp.concatenate([bias, bias], axis=0)
    mixed = []
    for head in range(heads):
        columns = slice(head * HD, (head + 1) * HD)
        query = jnp.concatenate([picked[0][:, columns], picked[1][:, columns]], axis=0)
        scores = dot_rows(query.astype(jnp.bfloat16), kv_buf[2 * head]) * (1.0 / math.sqrt(HD))
        scores = scores + bias
        weight = jnp.exp(scores - jnp.max(scores, axis=-1, keepdims=True))
        total = jnp.sum(weight, axis=-1, keepdims=True)
        mixture = dot32(weight.astype(jnp.bfloat16), kv_buf[2 * head + 1]) / total
        mixed.append(mixture.astype(jnp.bfloat16).astype(jnp.float32))
    result = jnp.concatenate(mixed, axis=1)
    for number in range(EXPERTS):
        block = jnp.zeros((rows, heads * HD), jnp.float32)
        for k in range(2):
            wanted = own_table[:, 1 + k : 2 + k]
            part = result[k * rows : (k + 1) * rows]
            block = block + jnp.where(wanted == float(number), part, 0.0)
        for part in range(holders):
            a_send[number * holders + part] = block[:, part * head_cols : (part + 1) * head_cols]
    a_recv[me] = a_send[me]
    arrive(send_req(3, lambda peer: a_send.at[peer], a_recv))

    def share_of(router):
        share = jnp.zeros((all_rows, 1), jnp.float32)
        for k in range(2):
            number = table[:, 1 + 2 * router + k : 2 + 2 * router + k]
            gate = table[:, 5 + 2 * router + k : 6 + 2 * router + k]
            share = share + jnp.where(number == expert, gate, 0.0)
        return share

    def project(values, weights, share, blocks):
        @pl.loop(0, half_width // 256)
        def _(index):
            offset = pl.multiple_of(index * 256, 256)
            left = dot32(values, weights[:, pl.ds(offset, 256)]) * share
            right = dot32(values, weights[:, pl.ds(half_width + offset, 256)]) * share
            both = jnp.concatenate(
                [left.reshape(count, rows, 256), right.reshape(count, rows, 256)], axis=1
            )
            blocks[:, :, pl.ds(offset, 256)] = both.astype(jnp.bfloat16)

    def combine(phase, rep_phase, blocks, landed, summed):
        landed[me] = blocks[me]
        arrive(send_req(phase, lambda peer: blocks.at[peer], landed))
        summed[rep] = jnp.sum(landed[...].astype(jnp.float32), axis=0).astype(jnp.bfloat16)
        arrive(send_rep(rep_phase, summed))
        return jnp.sum(summed[...].astype(jnp.float32), axis=0)

    answers = a_recv[...].reshape(all_rows, head_cols).astype(jnp.bfloat16)
    answers = dot32(moved_back, answers).astype(jnp.bfloat16)
    loads[1].wait()
    project(answers, wo, share_of(0), p_send1)
    hidden = inputs + combine(4, 0, p_send1, p_recv1, h_recv1)
    norm2[me] = half_norm(hidden, gain_ref[1])
    arrive(send_req(5, lambda peer: norm2.at[me], norm2))
    block_rows = whole_rows(norm2)
    loads[2].wait()
    loads[3].wait()

    @pl.loop(0, wg.shape[1] // 128)
    def _(index):
        span = pl.ds(pl.multiple_of(index * 128, 128), 128)
        both = dot32(block_rows, jnp.concatenate([wg[:, span], wu[:, span]], axis=1))
        gate_part, up_part = both[:, :128], both[:, 128:]
        units = gate_part / (1.0 + jnp.exp(-gate_part)) * up_part
        act_buf[:, span] = units.astype(jnp.bfloat16)

    loads[4].wait()
    project(act_buf[...], wd, share_of(1), p_send2)
    out_ref[...] = (hidden + combine(6, 1, p_send2, p_recv2, h_recv2)).astype(jnp.bfloat16)
    for copy in pending:
        copy.wait_send()


def shards(
    tokens,
    norm_gains,
    w_kv,
    w_query,
    w_out,
    w_gate,
    w_up,
    w_down,
    kv_pages,
    page_table,
    cache_len,
    route_ids,
    route_gates,
    new_slot,
):
    rows_dev, steps, width = tokens.shape
    rows = rows_dev * steps
    half_width = width // 2
    count = lax.axis_size("req")
    reps = lax.axis_size("rep")
    holders = count // EXPERTS
    pages, page, _, kv_cols = kv_pages.shape
    heads = kv_cols // HD
    positions = pages * page
    head_cols = w_query.shape[-1]
    units = w_gate.shape[-1]
    f32, bf16 = jnp.float32, jnp.bfloat16

    def interleaved(array, length):
        return array.reshape(length, 2, heads, HD).transpose(0, 2, 1, 3).reshape(-1, HD)

    halves = tokens.reshape(rows, 2, half_width).transpose(1, 0, 2).reshape(2 * rows, half_width)
    base = (lax.axis_index("req") * rows_dev + jnp.arange(rows_dev, dtype=jnp.int32)) * steps
    target = jnp.stack([base, new_slot * steps + 1], axis=1).reshape(rows, 1)
    ids = route_ids.transpose(0, 2, 1, 3).reshape(rows, 4)
    gates = route_gates.transpose(0, 2, 1, 3).reshape(rows, 4)
    meta = jnp.concatenate(
        [target.astype(f32), ids.astype(f32), gates.astype(f32), jnp.zeros((rows, 119), f32)],
        axis=1,
    )
    alive = pool_mask(page_table, cache_len, pages, page)
    alive = jnp.repeat(alive, steps, axis=0)
    place = jnp.arange(rows)[:, None]
    extra = jnp.arange(128)[None, :]
    extra_alive = (extra // steps == place // steps) & (extra <= place)
    bias = jnp.where(jnp.concatenate([alive, extra_alive], axis=1), 0.0, MASKED)

    any_spec = pl.BlockSpec(memory_space=pl.ANY)
    vmem_spec = pl.BlockSpec(memory_space=pltpu.VMEM)
    block = (count, 2 * rows, half_width)
    rep_block = (reps, 2 * rows, half_width)
    head_block = (count, rows, head_cols)
    scratch = [
        pltpu.VMEM((2 * heads, positions + 128, HD), bf16),
        pltpu.VMEM((2 * heads, width, HD), bf16),
        pltpu.VMEM((2, CHUNK, HD), bf16),
        pltpu.VMEM((CHUNK, HD), f32),
        pltpu.VMEM((width, head_cols), bf16),
        pltpu.VMEM((head_cols, width), bf16),
        pltpu.VMEM((width, units), bf16),
        pltpu.VMEM((width, units), bf16),
        pltpu.VMEM((units, width), bf16),
        pltpu.VMEM((count * rows, units), bf16),
        pltpu.VMEM(block, bf16),
        pltpu.VMEM((count, rows, 128), f32),
        pltpu.VMEM(head_block, f32),
        pltpu.VMEM(head_block, f32),
        pltpu.VMEM(head_block, f32),
        pltpu.VMEM(head_block, f32),
        pltpu.VMEM(block, bf16),
        pltpu.VMEM(block, bf16),
        pltpu.VMEM(rep_block, bf16),
        pltpu.VMEM(block, bf16),
        pltpu.VMEM(block, bf16),
        pltpu.VMEM(block, bf16),
        pltpu.VMEM(rep_block, bf16),
        pltpu.SemaphoreType.DMA((5,)),
        pltpu.SemaphoreType.DMA((2,)),
        pltpu.SemaphoreType.DMA((7, count)),
        pltpu.SemaphoreType.DMA((7, count)),
        pltpu.SemaphoreType.DMA((2, reps)),
        pltpu.SemaphoreType.DMA((2, reps)),
    ]
    out = pl.pallas_call(
        functools.partial(layer_kernel, holders),
        out_shape=jax.ShapeDtypeStruct((2 * rows, half_width), bf16),
        in_specs=[vmem_spec] * 4 + [any_spec] * 7,
        out_specs=vmem_spec,
        scratch_shapes=scratch,
        compiler_params=pltpu.CompilerParams(
            collective_id=0, has_side_effects=True, vmem_limit_bytes=58 * 1024 * 1024
        ),
    )(
        halves,
        norm_gains.reshape(2, 2, half_width),
        meta,
        bias,
        interleaved(kv_pages, positions),
        interleaved(w_kv, width),
        w_query[0],
        w_out[0],
        w_gate[0],
        w_up[0],
        w_down[0],
    )
    out = out.reshape(2, rows, half_width).transpose(1, 0, 2)
    return out.reshape(rows_dev, steps, width)


def solution(mesh):
    in_specs = (
        P("req", None, None),
        P(),
        P(None, None, "rep"),
        P("req", None, "rep"),
        P("req", "rep", None),
        P("req", None, "rep"),
        P("req", None, "rep"),
        P("req", "rep", None),
        P("req", None, None, "rep"),
        P("req", None),
        P("req"),
        P("req", None, None, None),
        P("req", None, None, None),
        P("req"),
    )
    out_specs = P("req", None, None)
    return jax.shard_map(shards, mesh=mesh, in_specs=in_specs, out_specs=out_specs, check_vma=False)
```

```python
import functools
import math

import jax
import jax.numpy as jnp
from jax import lax
from jax.experimental import pallas as pl
from jax.experimental.pallas import tpu as pltpu
from jax.sharding import PartitionSpec as P

HD = 128
EXPERTS = 8
EPSILON = 1e-06
MASKED = -1e30


CHUNK = 4096
MESH = pl.DeviceIdType.MESH


def dot32(left, right):
    return jnp.dot(left, right, preferred_element_type=jnp.float32)


def dot_rows(left, right):
    return lax.dot_general(left, right, (((1,), (1,)), ((), ())), preferred_element_type=jnp.float32)


def iota32(shape, dim):
    return lax.broadcasted_iota(jnp.int32, shape, dim).astype(jnp.float32)


def half_norm(values, gains):
    half = values.shape[0] // 2
    squares = jnp.sum(values * values, axis=-1, keepdims=True)
    mean = (squares[:half] + squares[half:]) / (2.0 * values.shape[1])
    scaling = lax.rsqrt(mean + EPSILON)
    width = values.shape[1]
    left = jnp.broadcast_to(gains[:, :width], (half, width))
    right = jnp.broadcast_to(gains[:, width:], (half, width))
    gain = jnp.concatenate([left, right], axis=0)
    return (values * jnp.concatenate([scaling, scaling], axis=0) * gain).astype(jnp.bfloat16)


def whole_rows(buffer):
    count, twice, half_width = buffer.shape
    rows = twice // 2
    wide = buffer[...].astype(jnp.float32)
    left = wide[:, :rows].reshape(count * rows, half_width)
    right = wide[:, rows:].reshape(count * rows, half_width)
    return jnp.concatenate([left, right], axis=1).astype(jnp.bfloat16)


def layer_kernel(
    holders,
    tok_ref,
    gain_ref,
    ids_ref,
    gates_ref,
    slot_ref,
    table_ref,
    length_ref,
    kv_ref,
    wkv_ref,
    wq_ref,
    wo_ref,
    wg_ref,
    wu_ref,
    wd_ref,
    out_ref,
    kv_buf,
    wkv_buf,
    kv_raw,
    wkv_raw,
    tok_buf,
    bias_buf,
    wq,
    wo,
    wg,
    wu,
    wd,
    act_buf,
    norm1,
    meta,
    q_send,
    q_recv,
    a_send,
    a_recv,
    p_send1,
    p_recv1,
    h_recv1,
    norm2,
    p_send2,
    p_recv2,
    h_recv2,
    weight_sem,
    kv_sem,
    wkv_sem,
    send_sem,
    recv_sem,
    rep_send_sem,
    rep_recv_sem,
):
    count = norm1.shape[0]
    reps = h_recv1.shape[0]
    rows = meta.shape[1]
    all_rows = count * rows
    half_width = norm1.shape[2]
    head_cols = wq.shape[1]
    heads = kv_buf.shape[0] // 2
    me = lax.axis_index("req")
    rep = lax.axis_index("rep")
    expert = (me // holders).astype(jnp.float32)
    pending = []

    loads = []
    for place, (source, target) in enumerate(
        ((wq_ref, wq), (wo_ref, wo), (wg_ref, wg), (wu_ref, wu), (wd_ref, wd))
    ):
        loads.append(pltpu.make_async_copy(source, target, weight_sem.at[place]))
    loads[0].start()
    kv_loads = []
    wkv_loads = []
    for source, target, sems, chunk_loads in (
        (kv_ref, kv_raw, kv_sem, kv_loads),
        (wkv_ref, wkv_raw, wkv_sem, wkv_loads),
    ):
        for index in range(source.shape[0] // CHUNK):
            part = pl.ds(index * CHUNK, CHUNK)
            load = pltpu.make_async_copy(source.at[part], target.at[part], sems.at[index])
            load.start()
            chunk_loads.append(load)

    barrier = pltpu.get_barrier_semaphore()
    for step in range(1, count):
        peer = lax.rem(me + step, count)
        pl.semaphore_signal(barrier, inc=1, device_id={"req": peer}, device_id_type=MESH)
    for step in range(1, reps):
        peer = lax.rem(rep + step, reps)
        pl.semaphore_signal(barrier, inc=1, device_id={"rep": peer}, device_id_type=MESH)

    def send_req(phase, block_of, target):
        copies = []
        for step in range(1, count):
            peer = lax.rem(me + step, count)
            copy = pltpu.make_async_remote_copy(
                src_ref=block_of(peer),
                dst_ref=target.at[me],
                send_sem=send_sem.at[phase, step],
                recv_sem=recv_sem.at[phase, step],
                device_id={"req": peer},
                device_id_type=MESH,
            )
            copy.start()
            copies.append(copy)
        pending.extend(copies)
        return copies

    def send_rep(phase, target):
        copies = []
        for step in range(1, reps):
            peer = lax.rem(rep + step, reps)
            copy = pltpu.make_async_remote_copy(
                src_ref=target.at[rep],
                dst_ref=target.at[rep],
                send_sem=rep_send_sem.at[phase, step],
                recv_sem=rep_recv_sem.at[phase, step],
                device_id={"rep": peer},
                device_id_type=MESH,
            )
            copy.start()
            copies.append(copy)
        pending.extend(copies)
        return copies

    def arrive(copies):
        for copy in copies:
            copy.wait_recv()

    spread_rows = 256
    per_piece = spread_rows // (2 * heads)
    line = lax.broadcasted_iota(jnp.int32, (spread_rows, spread_rows), 0)
    source_line = lax.rem(line, per_piece) * (2 * heads) + line // per_piece
    column = lax.broadcasted_iota(jnp.int32, (spread_rows, spread_rows), 1)
    sorter = jnp.where(source_line == column, 1.0, 0.0).astype(jnp.bfloat16)

    def split_chunk(raw, target, load, index):
        load.wait()
        pieces = [
            raw[pl.ds(index * CHUNK + spot * spread_rows, spread_rows), :]
            for spot in range(CHUNK // spread_rows)
        ]
        sorted_rows = dot32(sorter, jnp.concatenate(pieces, axis=1)).astype(jnp.bfloat16)
        per_chunk = CHUNK // (2 * heads)
        for part in range(2 * heads):
            block = sorted_rows[part * per_piece : (part + 1) * per_piece]
            for spot in range(CHUNK // spread_rows):
                start = index * per_chunk + spot * per_piece
                target[part, pl.ds(start, per_piece), :] = block[:, spot * HD : (spot + 1) * HD]

    def split_chunks(raw, target, chunk_loads, first, last):
        for index in range(first, last):
            split_chunk(raw, target, chunk_loads[index], index)

    for j in range(tok_ref.shape[0]):
        both = tok_ref[j].astype(jnp.float32)
        tok_buf[2 * j : 2 * j + 2, :] = both[:, :half_width]
        tok_buf[rows + 2 * j : rows + 2 * j + 2, :] = both[:, half_width:]
    inputs = tok_buf[...]
    norm1[me] = half_norm(inputs, gain_ref[0:1, :])

    line = lax.broadcasted_iota(jnp.int32, (rows, 128), 0)
    lane = lax.broadcasted_iota(jnp.int32, (rows, 128), 1)
    place = line * 128 + lane
    own = me * rows + line
    own_meta = jnp.where(lane == 0, own.astype(jnp.float32), 0.0)
    for j in range(rows // 2):
        moved_to = (slot_ref[j] * 2 + 1).astype(jnp.float32)
        own_meta = jnp.where(place == (2 * j + 1) * 128, moved_to, own_meta)
    for router in range(2):
        for step in range(2):
            numbers = ids_ref[router, step].astype(jnp.float32)
            weights = gates_ref[router, step].astype(jnp.float32)
            for k in range(2):
                for j in range(rows // 2):
                    spot = (2 * j + step) * 128 + 1 + 2 * router + k
                    number = numbers[k : k + 1, j : j + 1]
                    own_meta = jnp.where(place == spot, number, own_meta)
                    weight = weights[k : k + 1, j : j + 1]
                    own_meta = jnp.where(place == spot + 4, weight, own_meta)
    meta[me] = own_meta
    pl.semaphore_wait(barrier, count - 1 + reps - 1)
    norm_copies = send_req(0, lambda peer: norm1.at[me], norm1)
    meta_copies = send_req(1, lambda peer: meta.at[me], meta)
    for load in loads[1:]:
        load.start()

    kv_chunks = kv_ref.shape[0] // CHUNK
    wkv_chunks = wkv_ref.shape[0] // CHUNK
    pages = table_ref.shape[0] * table_ref.shape[1]
    page = (kv_buf.shape[1] - 128) // pages
    page_line = lax.broadcasted_iota(jnp.int32, (rows, pages), 0) // 2
    page_lane = lax.broadcasted_iota(jnp.int32, (rows, pages), 1)

    def place_page(index, held):
        for j in range(rows // 2):
            valid = jnp.clip(length_ref[j] - index * page, 0, page)
            here = (page_lane == table_ref[j, index]) & (page_line == j)
            held = jnp.where(here, valid, held)
        return held

    held = jnp.zeros((rows, pages), jnp.int32)
    held = lax.fori_loop(0, table_ref.shape[1], place_page, held)
    held = held.astype(jnp.float32).astype(jnp.bfloat16)
    span = 512
    span_line = lax.broadcasted_iota(jnp.int32, (pages, span), 0)
    span_page = lax.broadcasted_iota(jnp.int32, (pages, span), 1) // page
    within = lax.rem(lax.broadcasted_iota(jnp.int32, (rows, span), 1), page).astype(jnp.float32)
    for index in range(pages * page // span):
        widen = jnp.where(span_line == span_page + index * (span // page), 1.0, 0.0)
        wide = dot32(held, widen.astype(jnp.bfloat16))
        bias_buf[:, index * span : (index + 1) * span] = jnp.where(within < wide, 0.0, MASKED)
    extra_alive = (lane // 2 == line // 2) & (lane <= line)
    bias_buf[:, pages * page :] = jnp.where(extra_alive, 0.0, MASKED)
    split_chunks(kv_raw, kv_buf, kv_loads, 0, kv_chunks // 2)

    arrive(norm_copies)
    arrive(meta_copies)
    normed = whole_rows(norm1)
    table = meta[...].reshape(all_rows, 128)
    table16 = table.astype(jnp.bfloat16)
    moved = jnp.where(table[:, 0:1] == iota32((all_rows, all_rows), 1), 1.0, 0.0)
    moved = moved.astype(jnp.bfloat16)
    own_moved = jnp.where(own_meta[:, 0:1] == iota32((rows, all_rows), 1), 1.0, 0.0)
    own_moved = own_moved.astype(jnp.bfloat16)
    pick_lane = jnp.where(iota32((8, 128), 1) == 0.0, 1.0, 0.0).astype(jnp.bfloat16)
    target_row = dot_rows(pick_lane, table16)[0:1]
    moved_back = jnp.where(target_row == iota32((all_rows, all_rows), 0), 1.0, 0.0)
    moved_back = moved_back.astype(jnp.bfloat16)

    loads[0].wait()
    queries = dot32(normed, wq[...]).astype(jnp.bfloat16)
    q_send[...] = dot32(moved, queries).reshape(count, rows, head_cols)
    q_recv[me] = q_send[me]
    q_copies = send_req(2, lambda peer: q_send.at[peer], q_recv)

    split_chunks(wkv_raw, wkv_buf, wkv_loads, 0, wkv_chunks)
    own_rows = dot32(own_moved, normed).astype(jnp.bfloat16)
    own_table = dot32(own_moved, table16)
    for part in range(2 * heads):
        fresh = dot32(own_rows, wkv_buf[part])
        padded = jnp.concatenate([fresh, jnp.zeros((128 - rows, HD), jnp.float32)], axis=0)
        kv_buf[part, pl.ds(kv_buf.shape[1] - 128, 128), :] = padded.astype(jnp.bfloat16)
    split_chunks(kv_raw, kv_buf, kv_loads, kv_chunks // 2, kv_chunks)

    arrive(q_copies)
    picked = []
    for k in range(2):
        wanted = own_table[:, 1 + k : 2 + k]
        blocks = []
        for part in range(holders):
            block = jnp.zeros((rows, head_cols), jnp.float32)
            for number in range(EXPERTS):
                arrived = q_recv[number * holders + part]
                block = block + jnp.where(wanted == float(number), arrived, 0.0)
            blocks.append(block)
        picked.append(jnp.concatenate(blocks, axis=1) if holders > 1 else blocks[0])

    bias = bias_buf[...]
    bias = jnp.concatenate([bias, bias], axis=0)
    mixed = []
    for head in range(heads):
        columns = slice(head * HD, (head + 1) * HD)
        query = jnp.concatenate([picked[0][:, columns], picked[1][:, columns]], axis=0)
        scores = dot_rows(query.astype(jnp.bfloat16), kv_buf[2 * head]) * (1.0 / math.sqrt(HD))
        scores = scores + bias
        weight = jnp.exp(scores - jnp.max(scores, axis=-1, keepdims=True))
        total = jnp.sum(weight, axis=-1, keepdims=True)
        mixture = dot32(weight.astype(jnp.bfloat16), kv_buf[2 * head + 1]) / total
        mixed.append(mixture.astype(jnp.bfloat16).astype(jnp.float32))
    result = jnp.concatenate(mixed, axis=1)
    for number in range(EXPERTS):
        block = jnp.zeros((rows, heads * HD), jnp.float32)
        for k in range(2):
            wanted = own_table[:, 1 + k : 2 + k]
            part = result[k * rows : (k + 1) * rows]
            block = block + jnp.where(wanted == float(number), part, 0.0)
        for part in range(holders):
            a_send[number * holders + part] = block[:, part * head_cols : (part + 1) * head_cols]
    a_recv[me] = a_send[me]
    arrive(send_req(3, lambda peer: a_send.at[peer], a_recv))

    def share_of(router):
        share = jnp.zeros((all_rows, 1), jnp.float32)
        for k in range(2):
            number = table[:, 1 + 2 * router + k : 2 + 2 * router + k]
            gate = table[:, 5 + 2 * router + k : 6 + 2 * router + k]
            share = share + jnp.where(number == expert, gate, 0.0)
        return share

    def project(values, weights, share, blocks):
        @pl.loop(0, half_width // 256)
        def _(index):
            offset = pl.multiple_of(index * 256, 256)
            left = dot32(values, weights[:, pl.ds(offset, 256)]) * share
            right = dot32(values, weights[:, pl.ds(half_width + offset, 256)]) * share
            both = jnp.concatenate(
                [left.reshape(count, rows, 256), right.reshape(count, rows, 256)], axis=1
            )
            blocks[:, :, pl.ds(offset, 256)] = both.astype(jnp.bfloat16)

    def combine(phase, rep_phase, blocks, landed, summed):
        landed[me] = blocks[me]
        arrive(send_req(phase, lambda peer: blocks.at[peer], landed))
        summed[rep] = jnp.sum(landed[...].astype(jnp.float32), axis=0).astype(jnp.bfloat16)
        arrive(send_rep(rep_phase, summed))
        return jnp.sum(summed[...].astype(jnp.float32), axis=0)

    answers = a_recv[...].reshape(all_rows, head_cols).astype(jnp.bfloat16)
    answers = dot32(moved_back, answers).astype(jnp.bfloat16)
    loads[1].wait()
    project(answers, wo, share_of(0), p_send1)
    hidden = inputs + combine(4, 0, p_send1, p_recv1, h_recv1)
    norm2[me] = half_norm(hidden, gain_ref[1:2, :])
    arrive(send_req(5, lambda peer: norm2.at[me], norm2))
    block_rows = whole_rows(norm2)
    loads[2].wait()
    loads[3].wait()

    @pl.loop(0, wg.shape[1] // 128)
    def _(index):
        span = pl.ds(pl.multiple_of(index * 128, 128), 128)
        both = dot32(block_rows, jnp.concatenate([wg[:, span], wu[:, span]], axis=1))
        gate_part, up_part = both[:, :128], both[:, 128:]
        units = gate_part / (1.0 + jnp.exp(-gate_part)) * up_part
        act_buf[:, span] = units.astype(jnp.bfloat16)

    loads[4].wait()
    project(act_buf[...], wd, share_of(1), p_send2)
    final = hidden + combine(6, 1, p_send2, p_recv2, h_recv2)
    for j in range(out_ref.shape[0]):
        left = final[2 * j : 2 * j + 2]
        right = final[rows + 2 * j : rows + 2 * j + 2]
        out_ref[j] = jnp.concatenate([left, right], axis=1).astype(jnp.bfloat16)
    for copy in pending:
        copy.wait_send()


def shards(
    tokens,
    norm_gains,
    w_kv,
    w_query,
    w_out,
    w_gate,
    w_up,
    w_down,
    kv_pages,
    page_table,
    cache_len,
    route_ids,
    route_gates,
    new_slot,
):
    rows_dev, steps, width = tokens.shape
    rows = rows_dev * steps
    half_width = width // 2
    count = lax.axis_size("req")
    reps = lax.axis_size("rep")
    holders = count // EXPERTS
    pages, page, _, kv_cols = kv_pages.shape
    heads = kv_cols // HD
    positions = pages * page
    head_cols = w_query.shape[-1]
    units = w_gate.shape[-1]
    f32, bf16 = jnp.float32, jnp.bfloat16

    def interleaved(array, length):
        return array.reshape(length, 2, heads, HD).transpose(0, 2, 1, 3).reshape(-1, HD)

    any_spec = pl.BlockSpec(memory_space=pl.ANY)
    vmem_spec = pl.BlockSpec(memory_space=pltpu.VMEM)
    smem_spec = pl.BlockSpec(memory_space=pltpu.SMEM)
    block = (count, 2 * rows, half_width)
    rep_block = (reps, 2 * rows, half_width)
    head_block = (count, rows, head_cols)
    scratch = [
        pltpu.VMEM((2 * heads, positions + 128, HD), bf16),
        pltpu.VMEM((2 * heads, width, HD), bf16),
        pltpu.VMEM((positions * 2 * heads, HD), bf16),
        pltpu.VMEM((width * 2 * heads, HD), bf16),
        pltpu.VMEM((2 * rows, half_width), f32),
        pltpu.VMEM((rows, positions + 128), f32),
        pltpu.VMEM((width, head_cols), bf16),
        pltpu.VMEM((head_cols, width), bf16),
        pltpu.VMEM((width, units), bf16),
        pltpu.VMEM((width, units), bf16),
        pltpu.VMEM((units, width), bf16),
        pltpu.VMEM((count * rows, units), bf16),
        pltpu.VMEM(block, bf16),
        pltpu.VMEM((count, rows, 128), f32),
        pltpu.VMEM(head_block, f32),
        pltpu.VMEM(head_block, f32),
        pltpu.VMEM(head_block, f32),
        pltpu.VMEM(head_block, f32),
        pltpu.VMEM(block, bf16),
        pltpu.VMEM(block, bf16),
        pltpu.VMEM(rep_block, bf16),
        pltpu.VMEM(block, bf16),
        pltpu.VMEM(block, bf16),
        pltpu.VMEM(block, bf16),
        pltpu.VMEM(rep_block, bf16),
        pltpu.SemaphoreType.DMA((5,)),
        pltpu.SemaphoreType.DMA((positions * 2 * heads // CHUNK,)),
        pltpu.SemaphoreType.DMA((width * 2 * heads // CHUNK,)),
        pltpu.SemaphoreType.DMA((7, count)),
        pltpu.SemaphoreType.DMA((7, count)),
        pltpu.SemaphoreType.DMA((2, reps)),
        pltpu.SemaphoreType.DMA((2, reps)),
    ]
    out = pl.pallas_call(
        functools.partial(layer_kernel, holders),
        out_shape=jax.ShapeDtypeStruct((rows_dev, steps, width), bf16),
        in_specs=[vmem_spec] * 4 + [smem_spec] * 3 + [any_spec] * 7,
        out_specs=vmem_spec,
        scratch_shapes=scratch,
        compiler_params=pltpu.CompilerParams(
            collective_id=0, has_side_effects=True, vmem_limit_bytes=58 * 1024 * 1024
        ),
    )(
        tokens,
        norm_gains,
        route_ids.transpose(1, 2, 3, 0),
        route_gates.transpose(1, 2, 3, 0),
        new_slot,
        page_table,
        cache_len,
        interleaved(kv_pages, positions),
        interleaved(w_kv, width),
        w_query[0],
        w_out[0],
        w_gate[0],
        w_up[0],
        w_down[0],
    )
    return out


def solution(mesh):
    in_specs = (
        P("req", None, None),
        P(),
        P(None, None, "rep"),
        P("req", None, "rep"),
        P("req", "rep", None),
        P("req", None, "rep"),
        P("req", None, "rep"),
        P("req", "rep", None),
        P("req", None, None, "rep"),
        P("req", None),
        P("req"),
        P("req", None, None, None),
        P("req", None, None, None),
        P("req"),
    )
    out_specs = P("req", None, None)
    return jax.shard_map(shards, mesh=mesh, in_specs=in_specs, out_specs=out_specs, check_vma=False)
```

```python
import functools
import math

import jax
import jax.numpy as jnp
from jax import lax
from jax.experimental import pallas as pl
from jax.experimental.pallas import tpu as pltpu
from jax.sharding import PartitionSpec as P

HD = 128
EXPERTS = 8
EPSILON = 1e-06
MASKED = -1e30


CHUNK = 4096
COLUMN_PARTS = 2
MESH = pl.DeviceIdType.MESH


def dot32(left, right):
    return jnp.dot(left, right, preferred_element_type=jnp.float32)


def dot_rows(left, right):
    return lax.dot_general(left, right, (((1,), (1,)), ((), ())), preferred_element_type=jnp.float32)


def iota32(shape, dim):
    return lax.broadcasted_iota(jnp.int32, shape, dim).astype(jnp.float32)


def half_norm(values, gains):
    half = values.shape[0] // 2
    squares = jnp.sum(values * values, axis=-1, keepdims=True)
    mean = (squares[:half] + squares[half:]) / (2.0 * values.shape[1])
    scaling = lax.rsqrt(mean + EPSILON)
    width = values.shape[1]
    left = jnp.broadcast_to(gains[:, :width], (half, width))
    right = jnp.broadcast_to(gains[:, width:], (half, width))
    gain = jnp.concatenate([left, right], axis=0)
    return (values * jnp.concatenate([scaling, scaling], axis=0) * gain).astype(jnp.bfloat16)


def whole_rows(buffer):
    count, twice, half_width = buffer.shape
    rows = twice // 2
    wide = buffer[...].astype(jnp.float32)
    left = wide[:, :rows].reshape(count * rows, half_width)
    right = wide[:, rows:].reshape(count * rows, half_width)
    return jnp.concatenate([left, right], axis=1).astype(jnp.bfloat16)


def block_at(blocks, part, peer):
    return blocks.at[part, peer]


def layer_kernel(
    holders,
    tok_ref,
    gain_ref,
    ids_ref,
    gates_ref,
    slot_ref,
    table_ref,
    length_ref,
    kv_ref,
    wkv_ref,
    wq_ref,
    wo_ref,
    wg_ref,
    wu_ref,
    wd_ref,
    out_ref,
    kv_buf,
    kv_raw,
    wkv_raw,
    tok_buf,
    bias_buf,
    wq,
    wo,
    wg,
    wu,
    wd,
    act_buf,
    norm1,
    meta,
    q_send,
    q_recv,
    a_send,
    a_recv,
    p_send1,
    p_recv1,
    h_recv1,
    norm2,
    p_send2,
    p_recv2,
    h_recv2,
    weight_sem,
    kv_sem,
    wkv_sem,
    send_sem,
    recv_sem,
    rep_send_sem,
    rep_recv_sem,
):
    count = norm1.shape[0]
    reps = h_recv1.shape[1]
    rows = meta.shape[1]
    all_rows = count * rows
    half_width = norm1.shape[2]
    head_cols = wq.shape[1]
    heads = kv_buf.shape[0] // 2
    me = lax.axis_index("req")
    rep = lax.axis_index("rep")
    expert = (me // holders).astype(jnp.float32)
    pending = []

    loads = []
    for place, (source, target) in enumerate(
        ((wq_ref, wq), (wo_ref, wo), (wg_ref, wg), (wu_ref, wu), (wd_ref, wd))
    ):
        loads.append(pltpu.make_async_copy(source, target, weight_sem.at[place]))
    loads[0].start()
    kv_loads = []
    wkv_loads = []
    for source, target, sems, chunk_loads in (
        (kv_ref, kv_raw, kv_sem, kv_loads),
        (wkv_ref, wkv_raw, wkv_sem, wkv_loads),
    ):
        for index in range(source.shape[0] // CHUNK):
            part = pl.ds(index * CHUNK, CHUNK)
            load = pltpu.make_async_copy(source.at[part], target.at[part], sems.at[index])
            load.start()
            chunk_loads.append(load)

    barrier = pltpu.get_barrier_semaphore()
    for step in range(1, count):
        peer = lax.rem(me + step, count)
        pl.semaphore_signal(barrier, inc=1, device_id={"req": peer}, device_id_type=MESH)
    for step in range(1, reps):
        peer = lax.rem(rep + step, reps)
        pl.semaphore_signal(barrier, inc=1, device_id={"rep": peer}, device_id_type=MESH)

    def send_req(phase, block_of, target):
        copies = []
        for step in range(1, count):
            peer = lax.rem(me + step, count)
            copy = pltpu.make_async_remote_copy(
                src_ref=block_of(peer),
                dst_ref=target.at[me],
                send_sem=send_sem.at[phase, step],
                recv_sem=recv_sem.at[phase, step],
                device_id={"req": peer},
                device_id_type=MESH,
            )
            copy.start()
            copies.append(copy)
        pending.extend(copies)
        return copies

    def send_rep(phase, target):
        copies = []
        for step in range(1, reps):
            peer = lax.rem(rep + step, reps)
            copy = pltpu.make_async_remote_copy(
                src_ref=target.at[rep],
                dst_ref=target.at[rep],
                send_sem=rep_send_sem.at[phase, step],
                recv_sem=rep_recv_sem.at[phase, step],
                device_id={"rep": peer},
                device_id_type=MESH,
            )
            copy.start()
            copies.append(copy)
        pending.extend(copies)
        return copies

    def arrive(copies):
        for copy in copies:
            copy.wait_recv()

    spread_rows = 256
    per_piece = spread_rows // (2 * heads)
    line = lax.broadcasted_iota(jnp.int32, (spread_rows, spread_rows), 0)
    source_line = lax.rem(line, per_piece) * (2 * heads) + line // per_piece
    column = lax.broadcasted_iota(jnp.int32, (spread_rows, spread_rows), 1)
    sorter = jnp.where(source_line == column, 1.0, 0.0).astype(jnp.bfloat16)

    def split_chunk(raw, target, load, index):
        load.wait()
        pieces = [
            raw[pl.ds(index * CHUNK + spot * spread_rows, spread_rows), :]
            for spot in range(CHUNK // spread_rows)
        ]
        sorted_rows = dot32(sorter, jnp.concatenate(pieces, axis=1)).astype(jnp.bfloat16)
        per_chunk = CHUNK // (2 * heads)
        for part in range(2 * heads):
            block = sorted_rows[part * per_piece : (part + 1) * per_piece]
            for spot in range(CHUNK // spread_rows):
                start = index * per_chunk + spot * per_piece
                target[part, pl.ds(start, per_piece), :] = block[:, spot * HD : (spot + 1) * HD]

    def split_chunks(raw, target, chunk_loads, first, last):
        for index in range(first, last):
            split_chunk(raw, target, chunk_loads[index], index)

    for j in range(tok_ref.shape[0]):
        both = tok_ref[j].astype(jnp.float32)
        tok_buf[2 * j : 2 * j + 2, :] = both[:, :half_width]
        tok_buf[rows + 2 * j : rows + 2 * j + 2, :] = both[:, half_width:]
    inputs = tok_buf[...]
    norm1[me] = half_norm(inputs, gain_ref[0:1, :])

    line = lax.broadcasted_iota(jnp.int32, (rows, 128), 0)
    lane = lax.broadcasted_iota(jnp.int32, (rows, 128), 1)
    place = line * 128 + lane
    own = me * rows + line
    own_meta = jnp.where(lane == 0, own.astype(jnp.float32), 0.0)
    for j in range(rows // 2):
        moved_to = (slot_ref[j] * 2 + 1).astype(jnp.float32)
        own_meta = jnp.where(place == (2 * j + 1) * 128, moved_to, own_meta)
    for router in range(2):
        for step in range(2):
            numbers = ids_ref[router, step].astype(jnp.float32)
            weights = gates_ref[router, step].astype(jnp.float32)
            for k in range(2):
                for j in range(rows // 2):
                    spot = (2 * j + step) * 128 + 1 + 2 * router + k
                    number = numbers[k : k + 1, j : j + 1]
                    own_meta = jnp.where(place == spot, number, own_meta)
                    weight = weights[k : k + 1, j : j + 1]
                    own_meta = jnp.where(place == spot + 4, weight, own_meta)
    meta[me] = own_meta
    pl.semaphore_wait(barrier, count - 1 + reps - 1)
    norm_copies = send_req(0, lambda peer: norm1.at[me], norm1)
    meta_copies = send_req(1, lambda peer: meta.at[me], meta)
    for load in loads[1:]:
        load.start()

    kv_chunks = kv_ref.shape[0] // CHUNK
    pages = table_ref.shape[0] * table_ref.shape[1]
    page = (kv_buf.shape[1] - 128) // pages
    page_line = lax.broadcasted_iota(jnp.int32, (rows, pages), 0) // 2
    page_lane = lax.broadcasted_iota(jnp.int32, (rows, pages), 1)

    def place_page(index, held):
        for j in range(rows // 2):
            valid = jnp.clip(length_ref[j] - index * page, 0, page)
            here = (page_lane == table_ref[j, index]) & (page_line == j)
            held = jnp.where(here, valid, held)
        return held

    held = jnp.zeros((rows, pages), jnp.int32)
    held = lax.fori_loop(0, table_ref.shape[1], place_page, held)
    held = held.astype(jnp.float32).astype(jnp.bfloat16)
    span = 512
    span_line = lax.broadcasted_iota(jnp.int32, (pages, span), 0)
    span_page = lax.broadcasted_iota(jnp.int32, (pages, span), 1) // page
    within = lax.rem(lax.broadcasted_iota(jnp.int32, (rows, span), 1), page).astype(jnp.float32)
    for index in range(pages * page // span):
        widen = jnp.where(span_line == span_page + index * (span // page), 1.0, 0.0)
        wide = dot32(held, widen.astype(jnp.bfloat16))
        bias_buf[:, index * span : (index + 1) * span] = jnp.where(within < wide, 0.0, MASKED)
    extra_alive = (lane // 2 == line // 2) & (lane <= line)
    bias_buf[:, pages * page :] = jnp.where(extra_alive, 0.0, MASKED)
    split_chunks(kv_raw, kv_buf, kv_loads, 0, kv_chunks // 2)

    arrive(norm_copies)
    arrive(meta_copies)
    normed = whole_rows(norm1)
    table = meta[...].reshape(all_rows, 128)
    table16 = table.astype(jnp.bfloat16)
    moved = jnp.where(table[:, 0:1] == iota32((all_rows, all_rows), 1), 1.0, 0.0)
    moved = moved.astype(jnp.bfloat16)
    own_moved = jnp.where(own_meta[:, 0:1] == iota32((rows, all_rows), 1), 1.0, 0.0)
    own_moved = own_moved.astype(jnp.bfloat16)
    pick_lane = jnp.where(iota32((8, 128), 1) == 0.0, 1.0, 0.0).astype(jnp.bfloat16)
    target_row = dot_rows(pick_lane, table16)[0:1]
    moved_back = jnp.where(target_row == iota32((all_rows, all_rows), 0), 1.0, 0.0)
    moved_back = moved_back.astype(jnp.bfloat16)

    loads[0].wait()
    queries = dot32(normed, wq[...]).astype(jnp.bfloat16)
    q_send[...] = dot32(moved, queries).reshape(count, rows, head_cols)
    q_recv[me] = q_send[me]
    q_copies = send_req(2, lambda peer: q_send.at[peer], q_recv)

    own_rows = dot32(own_moved, normed)
    own_table = dot32(own_moved, table16)
    parts = 2 * heads
    tile_cols = 128 * parts
    tiles = own_rows.shape[1] // 128
    stacked = jnp.concatenate([own_rows[:, t * 128 : (t + 1) * 128] for t in range(tiles)], axis=0)
    repeat_line = lax.broadcasted_iota(jnp.int32, (128, tile_cols), 0)
    repeat_lane = lax.broadcasted_iota(jnp.int32, (128, tile_cols), 1) // parts
    repeater = jnp.where(repeat_line == repeat_lane, 1.0, 0.0).astype(jnp.bfloat16)
    repeated = dot32(stacked.astype(jnp.bfloat16), repeater)
    part_lane = lax.rem(lax.broadcasted_iota(jnp.int32, (rows, tile_cols), 1), parts)
    for load in wkv_loads:
        load.wait()
    fresh_all = jnp.zeros((parts * rows, HD), jnp.float32)
    for t in range(tiles):
        tile = repeated[t * rows : (t + 1) * rows]
        spread = [jnp.where(part_lane == part, tile, 0.0) for part in range(parts)]
        spread = jnp.concatenate(spread, axis=0).astype(jnp.bfloat16)
        fresh_all = fresh_all + dot32(spread, wkv_raw[t * tile_cols : (t + 1) * tile_cols, :])
    for part in range(parts):
        fresh = fresh_all[part * rows : (part + 1) * rows]
        padded = jnp.concatenate([fresh, jnp.zeros((128 - rows, HD), jnp.float32)], axis=0)
        kv_buf[part, pl.ds(kv_buf.shape[1] - 128, 128), :] = padded.astype(jnp.bfloat16)
    split_chunks(kv_raw, kv_buf, kv_loads, kv_chunks // 2, kv_chunks)

    arrive(q_copies)
    picked = []
    for k in range(2):
        wanted = own_table[:, 1 + k : 2 + k]
        blocks = []
        for part in range(holders):
            block = jnp.zeros((rows, head_cols), jnp.float32)
            for number in range(EXPERTS):
                arrived = q_recv[number * holders + part]
                block = block + jnp.where(wanted == float(number), arrived, 0.0)
            blocks.append(block)
        picked.append(jnp.concatenate(blocks, axis=1) if holders > 1 else blocks[0])

    bias = bias_buf[...]
    bias = jnp.concatenate([bias, bias], axis=0)
    mixed = []
    for head in range(heads):
        columns = slice(head * HD, (head + 1) * HD)
        query = jnp.concatenate([picked[0][:, columns], picked[1][:, columns]], axis=0)
        scores = dot_rows(query.astype(jnp.bfloat16), kv_buf[2 * head]) * (1.0 / math.sqrt(HD))
        scores = scores + bias
        weight = jnp.exp(scores - jnp.max(scores, axis=-1, keepdims=True))
        total = jnp.sum(weight, axis=-1, keepdims=True)
        mixture = dot32(weight.astype(jnp.bfloat16), kv_buf[2 * head + 1]) / total
        mixed.append(mixture.astype(jnp.bfloat16).astype(jnp.float32))
    result = jnp.concatenate(mixed, axis=1)
    for number in range(EXPERTS):
        block = jnp.zeros((rows, heads * HD), jnp.float32)
        for k in range(2):
            wanted = own_table[:, 1 + k : 2 + k]
            part = result[k * rows : (k + 1) * rows]
            block = block + jnp.where(wanted == float(number), part, 0.0)
        for part in range(holders):
            a_send[number * holders + part] = block[:, part * head_cols : (part + 1) * head_cols]
    a_recv[me] = a_send[me]
    arrive(send_req(3, lambda peer: a_send.at[peer], a_recv))

    def share_of(router):
        share = jnp.zeros((all_rows, 1), jnp.float32)
        for k in range(2):
            number = table[:, 1 + 2 * router + k : 2 + 2 * router + k]
            gate = table[:, 5 + 2 * router + k : 6 + 2 * router + k]
            share = share + jnp.where(number == expert, gate, 0.0)
        return share

    def project(values, weights, share, blocks, part):
        part_width = blocks.shape[3]

        @pl.loop(0, part_width // 256)
        def _(index):
            offset = pl.multiple_of(index * 256, 256)
            start = part * part_width + offset
            left = dot32(values, weights[:, pl.ds(start, 256)]) * share
            right = dot32(values, weights[:, pl.ds(half_width + start, 256)]) * share
            both = jnp.concatenate(
                [left.reshape(count, rows, 256), right.reshape(count, rows, 256)], axis=1
            )
            blocks[part, :, :, pl.ds(offset, 256)] = both.astype(jnp.bfloat16)

    def project_combine(values, weights, share, buffers, phase, rep_phase):
        blocks, landed, summed = buffers
        parts = range(blocks.shape[0])
        req_copies, rep_copies, totals = [], [], []
        for part in parts:
            project(values, weights, share, blocks, part)
            landed[part, me] = blocks[part, me]
            copies = send_req(
                phase + part, functools.partial(block_at, blocks, part), landed.at[part]
            )
            req_copies.append(copies)
        for part in parts:
            arrive(req_copies[part])
            total = jnp.sum(landed[part].astype(jnp.float32), axis=0)
            summed[part, rep] = total.astype(jnp.bfloat16)
            rep_copies.append(send_rep(rep_phase + part, summed.at[part]))
        for part in parts:
            arrive(rep_copies[part])
            totals.append(jnp.sum(summed[part].astype(jnp.float32), axis=0))
        return jnp.concatenate(totals, axis=1)

    answers = a_recv[...].reshape(all_rows, head_cols).astype(jnp.bfloat16)
    answers = dot32(moved_back, answers).astype(jnp.bfloat16)
    loads[1].wait()
    hidden = inputs + project_combine(
        answers, wo, share_of(0), (p_send1, p_recv1, h_recv1), 4, 0
    )
    norm2[me] = half_norm(hidden, gain_ref[1:2, :])
    arrive(send_req(4 + COLUMN_PARTS, lambda peer: norm2.at[me], norm2))
    block_rows = whole_rows(norm2)
    loads[2].wait()
    loads[3].wait()

    @pl.loop(0, wg.shape[1] // 128)
    def _(index):
        span = pl.ds(pl.multiple_of(index * 128, 128), 128)
        both = dot32(block_rows, jnp.concatenate([wg[:, span], wu[:, span]], axis=1))
        gate_part, up_part = both[:, :128], both[:, 128:]
        units = gate_part / (1.0 + jnp.exp(-gate_part)) * up_part
        act_buf[:, span] = units.astype(jnp.bfloat16)

    loads[4].wait()
    final = hidden + project_combine(
        act_buf[...],
        wd,
        share_of(1),
        (p_send2, p_recv2, h_recv2),
        5 + COLUMN_PARTS,
        COLUMN_PARTS,
    )
    for j in range(out_ref.shape[0]):
        left = final[2 * j : 2 * j + 2]
        right = final[rows + 2 * j : rows + 2 * j + 2]
        out_ref[j] = jnp.concatenate([left, right], axis=1)
    for copy in pending:
        copy.wait_send()


def shards(
    tokens,
    norm_gains,
    w_kv,
    w_query,
    w_out,
    w_gate,
    w_up,
    w_down,
    kv_pages,
    page_table,
    cache_len,
    route_ids,
    route_gates,
    new_slot,
):
    rows_dev, steps, width = tokens.shape
    rows = rows_dev * steps
    half_width = width // 2
    count = lax.axis_size("req")
    reps = lax.axis_size("rep")
    holders = count // EXPERTS
    pages, page, _, kv_cols = kv_pages.shape
    heads = kv_cols // HD
    positions = pages * page
    head_cols = w_query.shape[-1]
    units = w_gate.shape[-1]
    f32, bf16 = jnp.float32, jnp.bfloat16

    def interleaved(array, length):
        return array.reshape(length, 2, heads, HD).transpose(0, 2, 1, 3).reshape(-1, HD)

    any_spec = pl.BlockSpec(memory_space=pl.ANY)
    vmem_spec = pl.BlockSpec(memory_space=pltpu.VMEM)
    smem_spec = pl.BlockSpec(memory_space=pltpu.SMEM)
    block = (count, 2 * rows, half_width)
    part_block = (COLUMN_PARTS, count, 2 * rows, half_width // COLUMN_PARTS)
    rep_block = (COLUMN_PARTS, reps, 2 * rows, half_width // COLUMN_PARTS)
    head_block = (count, rows, head_cols)
    scratch = [
        pltpu.VMEM((2 * heads, positions + 128, HD), bf16),
        pltpu.VMEM((positions * 2 * heads, HD), bf16),
        pltpu.VMEM((width * 2 * heads, HD), bf16),
        pltpu.VMEM((2 * rows, half_width), f32),
        pltpu.VMEM((rows, positions + 128), f32),
        pltpu.VMEM((width, head_cols), bf16),
        pltpu.VMEM((head_cols, width), bf16),
        pltpu.VMEM((width, units), bf16),
        pltpu.VMEM((width, units), bf16),
        pltpu.VMEM((units, width), bf16),
        pltpu.VMEM((count * rows, units), bf16),
        pltpu.VMEM(block, bf16),
        pltpu.VMEM((count, rows, 128), f32),
        pltpu.VMEM(head_block, f32),
        pltpu.VMEM(head_block, f32),
        pltpu.VMEM(head_block, f32),
        pltpu.VMEM(head_block, f32),
        pltpu.VMEM(part_block, bf16),
        pltpu.VMEM(part_block, bf16),
        pltpu.VMEM(rep_block, bf16),
        pltpu.VMEM(block, bf16),
        pltpu.VMEM(part_block, bf16),
        pltpu.VMEM(part_block, bf16),
        pltpu.VMEM(rep_block, bf16),
        pltpu.SemaphoreType.DMA((5,)),
        pltpu.SemaphoreType.DMA((positions * 2 * heads // CHUNK,)),
        pltpu.SemaphoreType.DMA((width * 2 * heads // CHUNK,)),
        pltpu.SemaphoreType.DMA((5 + 2 * COLUMN_PARTS, count)),
        pltpu.SemaphoreType.DMA((5 + 2 * COLUMN_PARTS, count)),
        pltpu.SemaphoreType.DMA((2 * COLUMN_PARTS, reps)),
        pltpu.SemaphoreType.DMA((2 * COLUMN_PARTS, reps)),
    ]
    out = pl.pallas_call(
        functools.partial(layer_kernel, holders),
        out_shape=jax.ShapeDtypeStruct((rows_dev, steps, width), f32),
        in_specs=[vmem_spec] * 4 + [smem_spec] * 3 + [any_spec] * 7,
        out_specs=vmem_spec,
        scratch_shapes=scratch,
        compiler_params=pltpu.CompilerParams(
            collective_id=0, has_side_effects=True, vmem_limit_bytes=58 * 1024 * 1024
        ),
    )(
        tokens,
        norm_gains,
        route_ids.transpose(1, 2, 3, 0),
        route_gates.transpose(1, 2, 3, 0),
        new_slot,
        page_table,
        cache_len,
        interleaved(kv_pages, positions),
        interleaved(w_kv, width),
        w_query[0],
        w_out[0],
        w_gate[0],
        w_up[0],
        w_down[0],
    )
    return out.astype(bf16)


def solution(mesh):
    in_specs = (
        P("req", None, None),
        P(),
        P(None, None, "rep"),
        P("req", None, "rep"),
        P("req", "rep", None),
        P("req", None, "rep"),
        P("req", None, "rep"),
        P("req", "rep", None),
        P("req", None, None, "rep"),
        P("req", None),
        P("req"),
        P("req", None, None, None),
        P("req", None, None, None),
        P("req"),
    )
    out_specs = P("req", None, None)
    return jax.shard_map(shards, mesh=mesh, in_specs=in_specs, out_specs=out_specs, check_vma=False)
```

```python
import functools
import math

import jax
import jax.numpy as jnp
from jax import lax
from jax.experimental import pallas as pl
from jax.experimental.pallas import tpu as pltpu
from jax.sharding import PartitionSpec as P

HD = 128
EXPERTS = 8
EPSILON = 1e-06
MASKED = -1e30


CHUNK = 4096
COLUMN_PARTS = 2
MESH = pl.DeviceIdType.MESH


def dot32(left, right):
    return jnp.dot(left, right, preferred_element_type=jnp.float32)


def dot_rows(left, right):
    return lax.dot_general(left, right, (((1,), (1,)), ((), ())), preferred_element_type=jnp.float32)


def iota32(shape, dim):
    return lax.broadcasted_iota(jnp.int32, shape, dim).astype(jnp.float32)


def half_norm(values, gains):
    half = values.shape[0] // 2
    squares = jnp.sum(values * values, axis=-1, keepdims=True)
    mean = (squares[:half] + squares[half:]) / (2.0 * values.shape[1])
    scaling = lax.rsqrt(mean + EPSILON)
    width = values.shape[1]
    left = jnp.broadcast_to(gains[:, :width], (half, width))
    right = jnp.broadcast_to(gains[:, width:], (half, width))
    gain = jnp.concatenate([left, right], axis=0)
    return (values * jnp.concatenate([scaling, scaling], axis=0) * gain).astype(jnp.bfloat16)


def whole_rows(buffer):
    count, twice, half_width = buffer.shape
    rows = twice // 2
    wide = buffer[...].astype(jnp.float32)
    left = wide[:, :rows].reshape(count * rows, half_width)
    right = wide[:, rows:].reshape(count * rows, half_width)
    return jnp.concatenate([left, right], axis=1).astype(jnp.bfloat16)


def block_at(blocks, part, peer):
    return blocks.at[part, peer]


def layer_kernel(
    holders,
    tok_ref,
    gain_ref,
    ids_ref,
    gates_ref,
    slot_ref,
    table_ref,
    length_ref,
    kv_ref,
    wkv_ref,
    wq_ref,
    wo_ref,
    wg_ref,
    wu_ref,
    wd_ref,
    out_ref,
    kv_buf,
    kv_raw,
    wkv_raw,
    tok_buf,
    bias_buf,
    wq,
    wo,
    wg,
    wu,
    wd,
    act_buf,
    norm1,
    meta,
    q_send,
    q_recv,
    a_send,
    a_recv,
    p_send1,
    p_recv1,
    h_recv1,
    norm2,
    p_send2,
    p_recv2,
    h_recv2,
    weight_sem,
    kv_sem,
    wkv_sem,
    send_sem,
    recv_sem,
    rep_send_sem,
    rep_recv_sem,
):
    count = norm1.shape[0]
    reps = h_recv1.shape[1]
    rows = meta.shape[1]
    all_rows = count * rows
    half_width = norm1.shape[2]
    head_cols = wq.shape[1]
    heads = kv_buf.shape[0] // 2
    me = lax.axis_index("req")
    rep = lax.axis_index("rep")
    expert = (me // holders).astype(jnp.float32)
    pending = []

    loads = []
    for place, (source, target) in enumerate(
        ((wq_ref, wq), (wo_ref, wo), (wg_ref, wg), (wu_ref, wu), (wd_ref, wd))
    ):
        loads.append(pltpu.make_async_copy(source, target, weight_sem.at[place]))
    loads[0].start()
    kv_loads = []
    wkv_loads = []
    for source, target, sems, chunk_loads in (
        (kv_ref, kv_raw, kv_sem, kv_loads),
        (wkv_ref, wkv_raw, wkv_sem, wkv_loads),
    ):
        for index in range(source.shape[0] // CHUNK):
            part = pl.ds(index * CHUNK, CHUNK)
            load = pltpu.make_async_copy(source.at[part], target.at[part], sems.at[index])
            load.start()
            chunk_loads.append(load)

    barrier = pltpu.get_barrier_semaphore()
    for step in range(1, count):
        peer = lax.rem(me + step, count)
        pl.semaphore_signal(barrier, inc=1, device_id={"req": peer}, device_id_type=MESH)
    for step in range(1, reps):
        peer = lax.rem(rep + step, reps)
        pl.semaphore_signal(barrier, inc=1, device_id={"rep": peer}, device_id_type=MESH)

    def send_req(phase, block_of, target):
        copies = []
        for step in range(1, count):
            peer = lax.rem(me + step, count)
            copy = pltpu.make_async_remote_copy(
                src_ref=block_of(peer),
                dst_ref=target.at[me],
                send_sem=send_sem.at[phase, step],
                recv_sem=recv_sem.at[phase, step],
                device_id={"req": peer},
                device_id_type=MESH,
            )
            copy.start()
            copies.append(copy)
        pending.extend(copies)
        return copies

    def send_rep(phase, target):
        copies = []
        for step in range(1, reps):
            peer = lax.rem(rep + step, reps)
            copy = pltpu.make_async_remote_copy(
                src_ref=target.at[rep],
                dst_ref=target.at[rep],
                send_sem=rep_send_sem.at[phase, step],
                recv_sem=rep_recv_sem.at[phase, step],
                device_id={"rep": peer},
                device_id_type=MESH,
            )
            copy.start()
            copies.append(copy)
        pending.extend(copies)
        return copies

    def arrive(copies):
        for copy in copies:
            copy.wait_recv()

    spread_rows = 256
    per_piece = spread_rows // (2 * heads)
    line = lax.broadcasted_iota(jnp.int32, (spread_rows, spread_rows), 0)
    source_line = lax.rem(line, per_piece) * (2 * heads) + line // per_piece
    column = lax.broadcasted_iota(jnp.int32, (spread_rows, spread_rows), 1)
    sorter = jnp.where(source_line == column, 1.0, 0.0).astype(jnp.bfloat16)

    def split_chunk(raw, target, load, index):
        load.wait()
        per_chunk = CHUNK // (2 * heads)
        for pair in range(CHUNK // (2 * spread_rows)):
            pieces = [
                raw[pl.ds(index * CHUNK + (2 * pair + side) * spread_rows, spread_rows), :]
                for side in range(2)
            ]
            sorted_rows = dot32(sorter, jnp.concatenate(pieces, axis=1)).astype(jnp.bfloat16)
            for part in range(2 * heads):
                block = sorted_rows[part * per_piece : (part + 1) * per_piece]
                for side in range(2):
                    start = index * per_chunk + (2 * pair + side) * per_piece
                    target[part, pl.ds(start, per_piece), :] = block[:, side * HD : (side + 1) * HD]

    def split_chunks(raw, target, chunk_loads, first, last):
        for index in range(first, last):
            split_chunk(raw, target, chunk_loads[index], index)

    for j in range(tok_ref.shape[0]):
        both = tok_ref[j].astype(jnp.float32)
        tok_buf[2 * j : 2 * j + 2, :] = both[:, :half_width]
        tok_buf[rows + 2 * j : rows + 2 * j + 2, :] = both[:, half_width:]
    inputs = tok_buf[...]
    norm1[me] = half_norm(inputs, gain_ref[0:1, :])

    line = lax.broadcasted_iota(jnp.int32, (rows, 128), 0)
    lane = lax.broadcasted_iota(jnp.int32, (rows, 128), 1)
    place = line * 128 + lane
    own = me * rows + line
    own_meta = jnp.where(lane == 0, own.astype(jnp.float32), 0.0)
    for j in range(rows // 2):
        moved_to = (slot_ref[j] * 2 + 1).astype(jnp.float32)
        own_meta = jnp.where(place == (2 * j + 1) * 128, moved_to, own_meta)
    for router in range(2):
        for step in range(2):
            numbers = ids_ref[router, step].astype(jnp.float32)
            weights = gates_ref[router, step].astype(jnp.float32)
            for k in range(2):
                for j in range(rows // 2):
                    spot = (2 * j + step) * 128 + 1 + 2 * router + k
                    number = numbers[k : k + 1, j : j + 1]
                    own_meta = jnp.where(place == spot, number, own_meta)
                    weight = weights[k : k + 1, j : j + 1]
                    own_meta = jnp.where(place == spot + 4, weight, own_meta)
    meta[me] = own_meta
    pl.semaphore_wait(barrier, count - 1 + reps - 1)
    norm_copies = send_req(0, lambda peer: norm1.at[me], norm1)
    meta_copies = send_req(1, lambda peer: meta.at[me], meta)
    for load in loads[1:]:
        load.start()

    kv_chunks = kv_ref.shape[0] // CHUNK
    pages = table_ref.shape[0] * table_ref.shape[1]
    page = (kv_buf.shape[1] - 128) // pages
    page_line = lax.broadcasted_iota(jnp.int32, (rows, pages), 0) // 2
    page_lane = lax.broadcasted_iota(jnp.int32, (rows, pages), 1)

    def place_page(index, held):
        for j in range(rows // 2):
            valid = jnp.clip(length_ref[j] - index * page, 0, page)
            here = (page_lane == table_ref[j, index]) & (page_line == j)
            held = jnp.where(here, valid, held)
        return held

    held = jnp.zeros((rows, pages), jnp.int32)
    held = lax.fori_loop(0, table_ref.shape[1], place_page, held)
    held = held.astype(jnp.float32).astype(jnp.bfloat16)
    span = 512
    span_line = lax.broadcasted_iota(jnp.int32, (pages, span), 0)
    span_page = lax.broadcasted_iota(jnp.int32, (pages, span), 1) // page
    within = lax.rem(lax.broadcasted_iota(jnp.int32, (rows, span), 1), page).astype(jnp.float32)
    for index in range(pages * page // span):
        widen = jnp.where(span_line == span_page + index * (span // page), 1.0, 0.0)
        wide = dot32(held, widen.astype(jnp.bfloat16))
        bias_buf[:, index * span : (index + 1) * span] = jnp.where(within < wide, 0.0, MASKED)
    extra_alive = (lane // 2 == line // 2) & (lane <= line)
    bias_buf[:, pages * page :] = jnp.where(extra_alive, 0.0, MASKED)
    split_chunks(kv_raw, kv_buf, kv_loads, 0, kv_chunks // 2)

    arrive(norm_copies)
    arrive(meta_copies)
    normed = whole_rows(norm1)
    table = meta[...].reshape(all_rows, 128)
    table16 = table.astype(jnp.bfloat16)
    moved = jnp.where(table[:, 0:1] == iota32((all_rows, all_rows), 1), 1.0, 0.0)
    moved = moved.astype(jnp.bfloat16)
    own_moved = jnp.where(own_meta[:, 0:1] == iota32((rows, all_rows), 1), 1.0, 0.0)
    own_moved = own_moved.astype(jnp.bfloat16)
    pick_lane = jnp.where(iota32((8, 128), 1) == 0.0, 1.0, 0.0).astype(jnp.bfloat16)
    target_row = dot_rows(pick_lane, table16)[0:1]
    moved_back = jnp.where(target_row == iota32((all_rows, all_rows), 0), 1.0, 0.0)
    moved_back = moved_back.astype(jnp.bfloat16)

    loads[0].wait()
    queries = dot32(normed, wq[...]).astype(jnp.bfloat16)
    q_send[...] = dot32(moved, queries).reshape(count, rows, head_cols)
    q_recv[me] = q_send[me]
    q_copies = send_req(2, lambda peer: q_send.at[peer], q_recv)

    own_rows = dot32(own_moved, normed)
    own_table = dot32(own_moved, table16)
    parts = 2 * heads
    tile_cols = 128 * parts
    tiles = own_rows.shape[1] // 128
    stacked = jnp.concatenate([own_rows[:, t * 128 : (t + 1) * 128] for t in range(tiles)], axis=0)
    repeat_line = lax.broadcasted_iota(jnp.int32, (128, tile_cols), 0)
    repeat_lane = lax.broadcasted_iota(jnp.int32, (128, tile_cols), 1) // parts
    repeater = jnp.where(repeat_line == repeat_lane, 1.0, 0.0).astype(jnp.bfloat16)
    repeated = dot32(stacked.astype(jnp.bfloat16), repeater)
    part_lane = lax.rem(lax.broadcasted_iota(jnp.int32, (rows, tile_cols), 1), parts)
    for load in wkv_loads:
        load.wait()
    fresh_all = jnp.zeros((parts * rows, HD), jnp.float32)
    for t in range(tiles):
        tile = repeated[t * rows : (t + 1) * rows]
        spread = [jnp.where(part_lane == part, tile, 0.0) for part in range(parts)]
        spread = jnp.concatenate(spread, axis=0).astype(jnp.bfloat16)
        fresh_all = fresh_all + dot32(spread, wkv_raw[t * tile_cols : (t + 1) * tile_cols, :])
    for part in range(parts):
        fresh = fresh_all[part * rows : (part + 1) * rows]
        padded = jnp.concatenate([fresh, jnp.zeros((128 - rows, HD), jnp.float32)], axis=0)
        kv_buf[part, pl.ds(kv_buf.shape[1] - 128, 128), :] = padded.astype(jnp.bfloat16)
    split_chunks(kv_raw, kv_buf, kv_loads, kv_chunks // 2, kv_chunks)

    arrive(q_copies)
    picked = []
    for k in range(2):
        wanted = own_table[:, 1 + k : 2 + k]
        blocks = []
        for part in range(holders):
            block = jnp.zeros((rows, head_cols), jnp.float32)
            for number in range(EXPERTS):
                arrived = q_recv[number * holders + part]
                block = block + jnp.where(wanted == float(number), arrived, 0.0)
            blocks.append(block)
        picked.append(jnp.concatenate(blocks, axis=1) if holders > 1 else blocks[0])

    bias = bias_buf[...]
    bias = jnp.concatenate([bias, bias], axis=0)
    all_scores = []
    for head in range(heads):
        columns = slice(head * HD, (head + 1) * HD)
        query = jnp.concatenate([picked[0][:, columns], picked[1][:, columns]], axis=0)
        scores = dot_rows(query.astype(jnp.bfloat16), kv_buf[2 * head]) * (1.0 / math.sqrt(HD))
        all_scores.append(scores + bias)
    mixed = []
    for head in range(heads):
        scores = all_scores[head]
        weight = jnp.exp(scores - jnp.max(scores, axis=-1, keepdims=True))
        total = jnp.sum(weight, axis=-1, keepdims=True)
        mixture = dot32(weight.astype(jnp.bfloat16), kv_buf[2 * head + 1]) / total
        mixed.append(mixture.astype(jnp.bfloat16).astype(jnp.float32))
    result = jnp.concatenate(mixed, axis=1)
    for number in range(EXPERTS):
        block = jnp.zeros((rows, heads * HD), jnp.float32)
        for k in range(2):
            wanted = own_table[:, 1 + k : 2 + k]
            part = result[k * rows : (k + 1) * rows]
            block = block + jnp.where(wanted == float(number), part, 0.0)
        for part in range(holders):
            a_send[number * holders + part] = block[:, part * head_cols : (part + 1) * head_cols]
    a_recv[me] = a_send[me]
    arrive(send_req(3, lambda peer: a_send.at[peer], a_recv))

    def share_of(router):
        share = jnp.zeros((all_rows, 1), jnp.float32)
        for k in range(2):
            number = table[:, 1 + 2 * router + k : 2 + 2 * router + k]
            gate = table[:, 5 + 2 * router + k : 6 + 2 * router + k]
            share = share + jnp.where(number == expert, gate, 0.0)
        return share

    def project(values, weights, share, blocks, part):
        part_width = blocks.shape[3]

        @pl.loop(0, part_width // 256)
        def _(index):
            offset = pl.multiple_of(index * 256, 256)
            start = part * part_width + offset
            left = dot32(values, weights[:, pl.ds(start, 256)]) * share
            right = dot32(values, weights[:, pl.ds(half_width + start, 256)]) * share
            both = jnp.concatenate(
                [left.reshape(count, rows, 256), right.reshape(count, rows, 256)], axis=1
            )
            blocks[part, :, :, pl.ds(offset, 256)] = both.astype(jnp.bfloat16)

    def project_combine(values, weights, share, buffers, phase, rep_phase):
        blocks, landed, summed = buffers
        parts = range(blocks.shape[0])
        req_copies, rep_copies, totals = [], [], []
        for part in parts:
            project(values, weights, share, blocks, part)
            landed[part, me] = blocks[part, me]
            copies = send_req(
                phase + part, functools.partial(block_at, blocks, part), landed.at[part]
            )
            req_copies.append(copies)
        for part in parts:
            arrive(req_copies[part])
            total = jnp.sum(landed[part].astype(jnp.float32), axis=0)
            summed[part, rep] = total.astype(jnp.bfloat16)
            rep_copies.append(send_rep(rep_phase + part, summed.at[part]))
        for part in parts:
            arrive(rep_copies[part])
            totals.append(jnp.sum(summed[part].astype(jnp.float32), axis=0))
        return jnp.concatenate(totals, axis=1)

    answers = a_recv[...].reshape(all_rows, head_cols).astype(jnp.bfloat16)
    answers = dot32(moved_back, answers).astype(jnp.bfloat16)
    loads[1].wait()
    hidden = inputs + project_combine(
        answers, wo, share_of(0), (p_send1, p_recv1, h_recv1), 4, 0
    )
    norm2[me] = half_norm(hidden, gain_ref[1:2, :])
    arrive(send_req(4 + COLUMN_PARTS, lambda peer: norm2.at[me], norm2))
    block_rows = whole_rows(norm2)
    loads[2].wait()
    loads[3].wait()

    @pl.loop(0, wg.shape[1] // 128)
    def _(index):
        span = pl.ds(pl.multiple_of(index * 128, 128), 128)
        both = dot32(block_rows, jnp.concatenate([wg[:, span], wu[:, span]], axis=1))
        gate_part, up_part = both[:, :128], both[:, 128:]
        units = gate_part / (1.0 + jnp.exp(-gate_part)) * up_part
        act_buf[:, span] = units.astype(jnp.bfloat16)

    loads[4].wait()
    final = hidden + project_combine(
        act_buf[...],
        wd,
        share_of(1),
        (p_send2, p_recv2, h_recv2),
        5 + COLUMN_PARTS,
        COLUMN_PARTS,
    )
    for j in range(out_ref.shape[0]):
        left = final[2 * j : 2 * j + 2]
        right = final[rows + 2 * j : rows + 2 * j + 2]
        out_ref[j] = jnp.concatenate([left, right], axis=1)
    for copy in pending:
        copy.wait_send()


def shards(
    tokens,
    norm_gains,
    w_kv,
    w_query,
    w_out,
    w_gate,
    w_up,
    w_down,
    kv_pages,
    page_table,
    cache_len,
    route_ids,
    route_gates,
    new_slot,
):
    rows_dev, steps, width = tokens.shape
    rows = rows_dev * steps
    half_width = width // 2
    count = lax.axis_size("req")
    reps = lax.axis_size("rep")
    holders = count // EXPERTS
    pages, page, _, kv_cols = kv_pages.shape
    heads = kv_cols // HD
    positions = pages * page
    head_cols = w_query.shape[-1]
    units = w_gate.shape[-1]
    f32, bf16 = jnp.float32, jnp.bfloat16

    def interleaved(array, length):
        return array.reshape(length, 2, heads, HD).transpose(0, 2, 1, 3).reshape(-1, HD)

    any_spec = pl.BlockSpec(memory_space=pl.ANY)
    vmem_spec = pl.BlockSpec(memory_space=pltpu.VMEM)
    smem_spec = pl.BlockSpec(memory_space=pltpu.SMEM)
    block = (count, 2 * rows, half_width)
    part_block = (COLUMN_PARTS, count, 2 * rows, half_width // COLUMN_PARTS)
    rep_block = (COLUMN_PARTS, reps, 2 * rows, half_width // COLUMN_PARTS)
    head_block = (count, rows, head_cols)
    scratch = [
        pltpu.VMEM((2 * heads, positions + 128, HD), bf16),
        pltpu.VMEM((positions * 2 * heads, HD), bf16),
        pltpu.VMEM((width * 2 * heads, HD), bf16),
        pltpu.VMEM((2 * rows, half_width), f32),
        pltpu.VMEM((rows, positions + 128), f32),
        pltpu.VMEM((width, head_cols), bf16),
        pltpu.VMEM((head_cols, width), bf16),
        pltpu.VMEM((width, units), bf16),
        pltpu.VMEM((width, units), bf16),
        pltpu.VMEM((units, width), bf16),
        pltpu.VMEM((count * rows, units), bf16),
        pltpu.VMEM(block, bf16),
        pltpu.VMEM((count, rows, 128), f32),
        pltpu.VMEM(head_block, f32),
        pltpu.VMEM(head_block, f32),
        pltpu.VMEM(head_block, f32),
        pltpu.VMEM(head_block, f32),
        pltpu.VMEM(part_block, bf16),
        pltpu.VMEM(part_block, bf16),
        pltpu.VMEM(rep_block, bf16),
        pltpu.VMEM(block, bf16),
        pltpu.VMEM(part_block, bf16),
        pltpu.VMEM(part_block, bf16),
        pltpu.VMEM(rep_block, bf16),
        pltpu.SemaphoreType.DMA((5,)),
        pltpu.SemaphoreType.DMA((positions * 2 * heads // CHUNK,)),
        pltpu.SemaphoreType.DMA((width * 2 * heads // CHUNK,)),
        pltpu.SemaphoreType.DMA((5 + 2 * COLUMN_PARTS, count)),
        pltpu.SemaphoreType.DMA((5 + 2 * COLUMN_PARTS, count)),
        pltpu.SemaphoreType.DMA((2 * COLUMN_PARTS, reps)),
        pltpu.SemaphoreType.DMA((2 * COLUMN_PARTS, reps)),
    ]
    out = pl.pallas_call(
        functools.partial(layer_kernel, holders),
        out_shape=jax.ShapeDtypeStruct((rows_dev, steps, width), f32),
        in_specs=[vmem_spec] * 4 + [smem_spec] * 3 + [any_spec] * 7,
        out_specs=vmem_spec,
        scratch_shapes=scratch,
        compiler_params=pltpu.CompilerParams(
            collective_id=0, has_side_effects=True, vmem_limit_bytes=58 * 1024 * 1024
        ),
    )(
        tokens,
        norm_gains,
        route_ids.transpose(1, 2, 3, 0),
        route_gates.transpose(1, 2, 3, 0),
        new_slot,
        page_table,
        cache_len,
        interleaved(kv_pages, positions),
        interleaved(w_kv, width),
        w_query[0],
        w_out[0],
        w_gate[0],
        w_up[0],
        w_down[0],
    )
    return out.astype(bf16)


def solution(mesh):
    in_specs = (
        P("req", None, None),
        P(),
        P(None, None, "rep"),
        P("req", None, "rep"),
        P("req", "rep", None),
        P("req", None, "rep"),
        P("req", None, "rep"),
        P("req", "rep", None),
        P("req", None, None, "rep"),
        P("req", None),
        P("req"),
        P("req", None, None, None),
        P("req", None, None, None),
        P("req"),
    )
    out_specs = P("req", None, None)
    return jax.shard_map(shards, mesh=mesh, in_specs=in_specs, out_specs=out_specs, check_vma=False)
```
